256 devices in a mesh: dp: 4 (over y), seq: 16 (over z_lo, x, core), mp: 4 (over z_hi).
Axes of the slice: x: 4, y: 4, z: 8 (z_hi: 4, z_lo: 2; z = z_hi * 2 + z_lo), core: 2. Of those that a mesh axis runs over, the one named last changes fastest.
Arguments:
- queries: bfloat16 [4, 4096, 8192], P('dp', 'seq', 'mp'), may hold values from -300 to 300
- image_keys: bfloat16 [4, 16, 512, 1024], P('dp', 'seq', None, 'mp'), may hold values from -300 to 300
- image_values: bfloat16 [4, 16, 512, 1024], P('dp', 'seq', None, 'mp'), may hold values from -6 to 6
- norm_gains: float32 [2, 128], replicated, may hold values from 0.25 to 5
- image_tiles: int32 [4, 16], P('dp'), may hold values from 1 to 4, as said below
- read_mask: int32 [4, 32, 16], P('dp'), may hold values from 0 to 1, as said below
- grad_attended: bfloat16 [4, 4096, 8192], P('dp', 'seq', 'mp'), may hold values from -15 to 15
Outputs:
- attended: bfloat16 [4, 4096, 8192], P('dp', 'seq', 'mp')
- grad_queries: bfloat16 [4, 4096, 8192], P('dp', 'seq', 'mp')
- grad_keys: bfloat16 [4, 16, 512, 1024], P('dp', 'seq', None, 'mp')
- grad_values: bfloat16 [4, 16, 512, 1024], P('dp', 'seq', None, 'mp')
- grad_gains: float32 [2, 128], replicated
The draws below stay inside these ranges and needn't reach their ends.
Inputs may be any that keep to these rules, and one draw needn't show every extreme that they name: `image_tiles`: each document has an image of 4 tiles and an image of 1 tile. `read_mask`: each text tile reads 1 to 3 images with consecutive indices; the last text tile of each document reads exactly 3.
All inputs are finite; a program needn't handle non-finite values.
Results may differ from the reference program's by a relative error of at most 0.03.
The reference program's roundings to bfloat16 on the way count: a program that leaves them out, or rounds other values in their place, can miss the bound.
Values may be sent and summed in bfloat16 or wider, within the bound.
A program may use at most 192 MiB of HBM per device.

```python
import math
import jax
import jax.numpy as jnp
from jax import lax

HEADS = 64
KV_HEADS = 8
HEAD_DIM = 128
TEXT_TILE = 128
TILE_TOK = 128
MAX_TILES = 4
DOCS = 4
TOKENS = 4096
TILES = 32
IMAGES = 16
READS = 3
GROUP = 8
HD = 8192
KVD = 1024
MAXTOK = 512


def spread_scale(key, scale_shape, ratio):
    return jnp.exp(jax.random.uniform(key, scale_shape, jnp.float32, 0.0, math.log(ratio)))


def draw_queries(key, part):
    key = jax.random.fold_in(key, 11)
    key_base, key_rows, key_cols = jax.random.split(key, 3)
    full_shape = (DOCS, TOKENS, HD)
    noise_part = jnp.clip(jax.random.normal(key_base, full_shape, jnp.float32), -3.0, 3.0)
    return (noise_part * spread_scale(key_rows, (DOCS, TOKENS, 1), 10.0) * spread_scale(key_cols, (HD,), 10.0)).astype(jnp.bfloat16)


def draw_image_keys(key, part):
    key = jax.random.fold_in(key, 12)
    key_base, key_rows, key_cols = jax.random.split(key, 3)
    full_shape = (DOCS, IMAGES, MAXTOK, KVD)
    noise_part = jnp.clip(jax.random.normal(key_base, full_shape, jnp.float32), -3.0, 3.0)
    return (noise_part * spread_scale(key_rows, (DOCS, IMAGES, MAXTOK, 1), 10.0) * spread_scale(key_cols, (KVD,), 10.0)).astype(jnp.bfloat16)


def draw_norm_gains(key, part):
    key = jax.random.fold_in(key, 13)
    return jnp.exp(jax.random.uniform(key, (2, HEAD_DIM), jnp.float32, math.log(0.25), math.log(2.5)))


def draw_grad_attended(key, part):
    key = jax.random.fold_in(key, 14)
    key_base = jax.random.fold_in(key, 0)
    full_shape = (DOCS, TOKENS, HD)
    head_rank = (jnp.arange(HD) // HEAD_DIM).astype(jnp.float32)
    col_scale = 1.0 + 2.0 * head_rank / (HEADS - 1)
    return (jnp.clip(jax.random.normal(key_base, full_shape, jnp.float32), -4.0, 4.0) * col_scale).astype(jnp.bfloat16)


def draw_image_tiles(key, part):
    key = jax.random.fold_in(key, 15)
    key_tiles, key_most, key_least = jax.random.split(key, 3)
    counts = jax.random.randint(key_tiles, (DOCS, IMAGES), 1, MAX_TILES + 1)
    most_index = jax.random.randint(key_most, (DOCS,), 0, IMAGES)
    least_index = (most_index + 1 + jax.random.randint(key_least, (DOCS,), 0, IMAGES - 1)) % IMAGES
    image_ids = jnp.arange(IMAGES)[None, :]
    counts = jnp.where(image_ids == least_index[:, None], 1, counts)
    counts = jnp.where(image_ids == most_index[:, None], MAX_TILES, counts)
    return counts.astype(jnp.int32)


def draw_read_mask(key, part):
    key = jax.random.fold_in(key, 16)
    key_start, key_reads = jax.random.split(key, 2)
    image_ids = jnp.arange(IMAGES)
    tile_ids = jnp.arange(TILES)
    starts = jnp.sort(jax.random.randint(key_start, (DOCS, IMAGES), 0, TILES), axis=1)
    starts = jnp.where(image_ids[None, :] == 0, 0, starts)
    begun = starts[:, None, :] <= tile_ids[None, :, None]
    begun_count = jnp.sum(begun.astype(jnp.int32), axis=2)
    wanted = jax.random.randint(key_reads, (DOCS, TILES), 1, READS + 1)
    last_tile = tile_ids[None, :] == TILES - 1
    wanted = jnp.where(last_tile, READS, wanted)
    far_end = max(IMAGES // 2 - 1, READS - 1)
    window_end = jnp.where(last_tile, far_end, begun_count - 1)
    reading = begun & (image_ids[None, None, :] <= window_end[:, :, None]) & (image_ids[None, None, :] >= (window_end - wanted + 1)[:, :, None])
    return reading.astype(jnp.int32)


def shard_levels(rng, shape, shards, low, top_value):
    def one(dim, parts):
        heights = jax.random.uniform(jax.random.fold_in(jax.random.fold_in(rng, 6), dim), (parts,), jnp.float32, low / len(shards), top_value / len(shards))
        return jnp.repeat(jnp.exp(heights), shape[dim] // parts).reshape((-1,) + (1,) * (len(shape) - dim - 1))

    factor_of = one(*shards[0])
    for cut in shards[1:]:
        factor_of = factor_of * one(*cut)
    return factor_of


def centred(rng, dims, width, bound, shards=(), kind=jnp.bfloat16):
    factor_of = shard_levels(rng, dims, shards, -0.22, 0.18) if shards else 1.0
    values = jax.random.normal(rng, dims, jnp.float32) * width * factor_of
    return jnp.minimum(jnp.maximum(values, -bound), bound).astype(kind)


def setup_inputs(seed: int = 0) -> dict:
    key_of = jax.random.split(jax.random.key(seed), 8)
    queries = draw_queries(jax.random.fold_in(key_of[7], 71), 0)
    image_keys = draw_image_keys(jax.random.fold_in(key_of[7], 71), 0)
    image_values = centred(key_of[2], (DOCS, IMAGES, MAXTOK, KVD), 1.0, 6.0, ((0, 4), (1, 16), (3, 4)))
    norm_gains = draw_norm_gains(jax.random.fold_in(key_of[7], 71), 0)
    image_tiles = draw_image_tiles(jax.random.fold_in(key_of[7], 71), 0)
    read_mask = draw_read_mask(jax.random.fold_in(key_of[7], 71), 0)
    grad_attended = draw_grad_attended(jax.random.fold_in(key_of[7], 71), 0)
    return dict(queries=queries, image_keys=image_keys, image_values=image_values, norm_gains=norm_gains, image_tiles=image_tiles, read_mask=read_mask, grad_attended=grad_attended)


EPSILON = 1e-05

def read_slots(read_rows, tile_counts, slot_total):
    ranking = (jnp.cumsum(read_rows, axis=1) - 1).astype(jnp.int32)
    slot_ids = jnp.arange(slot_total, dtype=jnp.int32)
    matches = (read_rows[:, None, :] == 1) & (ranking[:, None, :] == slot_ids[None, :, None])
    match_int = matches.astype(jnp.int32)
    image_ids = jnp.arange(read_rows.shape[1], dtype=jnp.int32)
    chosen = lax.optimization_barrier(jnp.sum(match_int * image_ids[None, None, :], axis=2)).astype(jnp.int32)
    lengths = (tile_counts * TILE_TOK).astype(jnp.int32)
    slot_length = lax.optimization_barrier(jnp.sum(match_int * lengths[None, None, :], axis=2)).astype(jnp.int32)
    return (chosen, slot_length, matches)

def unit_rows(entries):
    inverse = lax.rsqrt(lax.optimization_barrier(jnp.mean(entries * entries, axis=-1, keepdims=True)) + EPSILON)
    return (entries * inverse, inverse)

def norm_backward(normed_grads, unit_part, inverse, gain_row):
    scaled = normed_grads * gain_row
    return inverse * (scaled - unit_part * lax.optimization_barrier(jnp.mean(scaled * unit_part, axis=-1, keepdims=True)))

def attend_group(query_group, cotangent_group, key_head, value_head, norm_gains, chosen, slot_length, match_float):
    score_scale = HEAD_DIM ** (-0.5)
    slot_width = READS * MAXTOK
    key_unit, key_inverse = unit_rows(key_head.astype(jnp.float32))
    key_normed = lax.optimization_barrier((key_unit * norm_gains[1]).astype(jnp.bfloat16))
    key_rows = key_normed[chosen].reshape(TILES, slot_width, HEAD_DIM).astype(jnp.float32)
    value_rows = value_head[chosen].reshape(TILES, slot_width, HEAD_DIM).astype(jnp.float32)
    key_index = jnp.arange(MAXTOK, dtype=jnp.int32)
    allowed = (key_index[None, None, :] < slot_length[:, :, None]).reshape(TILES, 1, slot_width)

    def one_query(query_items):
        query_head, cotangent_head = query_items
        query_unit, query_inverse = unit_rows(query_head.astype(jnp.float32))
        query_normed = lax.optimization_barrier((query_unit * norm_gains[0]).astype(jnp.bfloat16))
        query_tiles = query_normed.reshape(TILES, TEXT_TILE, HEAD_DIM).astype(jnp.float32)
        cotangent_tiles = cotangent_head.reshape(TILES, TEXT_TILE, HEAD_DIM).astype(jnp.float32)
        scores = jnp.einsum('tqd,tkd->tqk', query_tiles, key_rows) * score_scale
        masked = jnp.where(allowed, scores, -1e+30)
        row_peak = lax.optimization_barrier(jnp.max(masked, axis=2, keepdims=True))
        exponent = jnp.where(allowed, jnp.exp(masked - row_peak), 0.0)
        weights = lax.optimization_barrier((exponent / lax.optimization_barrier(jnp.sum(exponent, axis=2, keepdims=True))).astype(jnp.bfloat16))
        weight_values = weights.astype(jnp.float32)
        attended = jnp.einsum('tqk,tkd->tqd', weight_values, value_rows).astype(jnp.bfloat16).reshape(TOKENS, HEAD_DIM)
        value_scores = jnp.einsum('tqd,tkd->tqk', cotangent_tiles, value_rows)
        row_dot = lax.optimization_barrier(jnp.sum(weight_values * value_scores, axis=2, keepdims=True))
        score_grads = lax.optimization_barrier((weight_values * (value_scores - row_dot)).astype(jnp.bfloat16)).astype(jnp.float32)
        query_grads = (jnp.einsum('tqk,tkd->tqd', score_grads, key_rows) * score_scale).reshape(TOKENS, HEAD_DIM)
        key_slots = (jnp.einsum('tqk,tqd->tkd', score_grads, query_tiles) * score_scale).reshape(TILES, READS, MAXTOK, HEAD_DIM)
        value_slots = jnp.einsum('tqk,tqd->tkd', weight_values, cotangent_tiles).reshape(TILES, READS, MAXTOK, HEAD_DIM)
        key_part = jnp.einsum('tri,trkd->ikd', match_float, key_slots)
        value_part = jnp.einsum('tri,trkd->ikd', match_float, value_slots)
        grad_query = norm_backward(query_grads, query_unit, query_inverse, norm_gains[0]).astype(jnp.bfloat16)
        query_gain = lax.optimization_barrier(jnp.sum(query_grads * query_unit, axis=0))
        return (attended, grad_query, key_part, value_part, query_gain)
    attended, grad_query, key_parts, value_parts, query_gains = lax.map(one_query, (query_group, cotangent_group))
    key_grads = lax.optimization_barrier(jnp.sum(key_parts, axis=0))
    grad_key = norm_backward(key_grads, key_unit, key_inverse, norm_gains[1]).astype(jnp.bfloat16)
    grad_value = lax.optimization_barrier(jnp.sum(value_parts, axis=0)).astype(jnp.bfloat16)
    gain_terms = jnp.stack([lax.optimization_barrier(jnp.sum(query_gains, axis=0)), lax.optimization_barrier(jnp.sum(key_grads * key_unit, axis=(0, 1)))])
    return (attended, grad_query, grad_key, grad_value, gain_terms)

def reference(queries, image_keys, image_values, norm_gains, image_tiles, read_mask, grad_attended):

    def one_document(document):
        query_doc, key_doc, value_doc, tile_doc, mask_doc, cotangent_doc = document
        chosen, slot_length, matches = read_slots(mask_doc, tile_doc, READS)
        match_float = matches.astype(jnp.float32)
        query_kv = jnp.transpose(query_doc.reshape(TOKENS, KV_HEADS, GROUP, HEAD_DIM), (1, 2, 0, 3))
        cotangent_kv = jnp.transpose(cotangent_doc.reshape(TOKENS, KV_HEADS, GROUP, HEAD_DIM), (1, 2, 0, 3))
        key_kv = jnp.transpose(key_doc.reshape(IMAGES, MAXTOK, KV_HEADS, HEAD_DIM), (2, 0, 1, 3))
        value_kv = jnp.transpose(value_doc.reshape(IMAGES, MAXTOK, KV_HEADS, HEAD_DIM), (2, 0, 1, 3))

        def one_group(group_items):
            query_group, cotangent_group, key_head, value_head = group_items
            return attend_group(query_group, cotangent_group, key_head, value_head, norm_gains, chosen, slot_length, match_float)
        attended, grad_query, grad_key, grad_value, gain_terms = lax.map(one_group, (query_kv, cotangent_kv, key_kv, value_kv))
        return (jnp.transpose(attended, (2, 0, 1, 3)).reshape(TOKENS, HD), jnp.transpose(grad_query, (2, 0, 1, 3)).reshape(TOKENS, HD), jnp.transpose(grad_key, (1, 2, 0, 3)).reshape(IMAGES, MAXTOK, KVD), jnp.transpose(grad_value, (1, 2, 0, 3)).reshape(IMAGES, MAXTOK, KVD), lax.optimization_barrier(jnp.sum(gain_terms, axis=0)))
    doc_results = lax.map(one_document, (queries, image_keys, image_values, image_tiles, read_mask, grad_attended))
    attended, grad_queries, grad_keys, grad_values, gain_docs = doc_results
    return (attended, grad_queries, grad_keys, grad_values, lax.optimization_barrier(jnp.sum(gain_docs, axis=0)))
```

```python
import functools

import jax
import jax.numpy as jnp
from jax import lax
from jax.experimental import pallas as pl
from jax.experimental.pallas import tpu as pltpu
from jax.sharding import PartitionSpec as P

HEAD_DIM = 128
TEXT_TILE = 128
TILE_TOK = 128
READ_MOST = 3
EPSILON = 1e-05
LOG2E = 1.4426950408889634
MESH = pl.DeviceIdType.MESH
BF16 = jnp.bfloat16
F32 = jnp.float32

RING = 4


def dot(a, b):
    return jnp.dot(a, b, preferred_element_type=F32)


def kernel(
    images,
    group,
    q_ref,
    do_ref,
    k_ref,
    v_ref,
    gains_ref,
    tiles_ref,
    mask_ref,
    o_out,
    dq_out,
    dk_out,
    dv_out,
    gain_out,
    q4,
    do4,
    kraw,
    kbuf,
    vbuf,
    qn,
    qnt,
    dot_t,
    don,
    ut,
    rinv,
    wbuf,
    sbuf,
    vslot,
    kslot,
    vsend,
    ksend,
    vland,
    kland,
    obuf,
    dqbuf,
    gkbuf,
    gvbuf,
    qgain,
    gcol,
    local_sem,
    swap_send,
    swap_recv,
    ag_send,
    ag_recv,
    rs_send,
    rs_recv,
    out_local,
    out_send,
    out_recv,
):
    max_tokens = k_ref.shape[0]
    tokens = q_ref.shape[0]
    half = group * HEAD_DIM
    pair_width = 2 * HEAD_DIM
    pairs = group // 2
    tile_total = 2 * tokens // TEXT_TILE
    subs = max_tokens // TILE_TOK
    scale = HEAD_DIM ** (-0.5)

    seq = lax.axis_index("seq")
    core = lax.rem(seq, 2)
    x = lax.rem(lax.div(seq, 2), RING)
    z = lax.div(seq, 2 * RING)
    other = 1 - core

    def image_at(zz, xx, parity):
        return zz * (2 * RING) + lax.rem(xx + RING, RING) * 2 + parity

    peer = image_at(z, x, other)
    right = image_at(z, x + 1, core)
    left = image_at(z, x - 1, core)
    across = image_at(1 - z, x, core)
    chip = image_at(z, x, 0)

    def columns(index, width):
        return pl.ds(pl.multiple_of(index * width, width), width)

    own_rows = columns(core, tokens)
    other_rows = columns(other, tokens)

    def remote(src, dst, send_sem, recv_sem, device):
        return pltpu.make_async_remote_copy(
            src_ref=src,
            dst_ref=dst,
            send_sem=send_sem,
            recv_sem=recv_sem,
            device_id={"seq": device},
            device_id_type=MESH,
        )

    mine = [
        pltpu.make_async_copy(k_ref.at[:, columns(core, HEAD_DIM)], kraw.at[core], local_sem.at[0]),
        pltpu.make_async_copy(
            v_ref.at[:, columns(core, HEAD_DIM)], vbuf.at[chip + core], local_sem.at[1]
        ),
        pltpu.make_async_copy(q_ref.at[:, columns(core, half)], q4.at[own_rows], local_sem.at[2]),
        pltpu.make_async_copy(do_ref.at[:, columns(core, half)], do4.at[own_rows], local_sem.at[3]),
    ]
    for copy in mine:
        copy.start()

    barrier = pltpu.get_barrier_semaphore()
    for device in (peer, right, left, across):
        pl.semaphore_signal(barrier, inc=1, device_id={"seq": device}, device_id_type=MESH)
    pl.semaphore_wait(barrier, 4)

    swaps = [
        (k_ref.at[:, columns(other, HEAD_DIM)], kraw.at[core]),
        (v_ref.at[:, columns(other, HEAD_DIM)], vbuf.at[chip + core]),
        (q_ref.at[:, columns(other, half)], q4.at[own_rows]),
        (do_ref.at[:, columns(other, half)], do4.at[own_rows]),
    ]
    swaps = [
        remote(src, dst, swap_send.at[i], swap_recv.at[i], peer)
        for i, (src, dst) in enumerate(swaps)
    ]
    for copy in swaps:
        copy.start()

    tile_base = lax.div(seq, 2) * tile_total
    first, count = [], []
    for t in range(tile_total):
        begin = jnp.int32(images)
        total = jnp.int32(0)
        for i in range(images):
            flag = mask_ref[tile_base + t, i]
            total = total + flag
            begin = jnp.where((flag == 1) & (begin == images), i, begin)
        first.append(begin)
        count.append(total)

    def pick(values, t):
        out = values[0]
        for k in range(1, len(values)):
            out = jnp.where(t == k, values[k], out)
        return out

    def reads(t):
        begin = pick(first, t)
        total = pick(count, t)
        found = []
        for r in range(READ_MOST):
            image = jnp.minimum(begin + r, images - 1)
            length = jnp.where(r < total, tiles_ref[image] * TILE_TOK, 0)
            found.append((image, length))
        return found

    def gather_copy(buf, which, number, parity):
        if number == 6:
            image, device = image_at(z, x, parity), right
        elif number == 7:
            image, device = image_at(z, x, parity), left
        elif number == 4:
            image, device = image_at(z, x, parity), across
        elif number == 5 and parity == 0:
            image, device = image_at(z, x - 1, 0), right
        elif number == 5:
            image, device = image_at(z, x + 1, 1), left
        elif number == 1:
            image, device = image_at(1 - z, x, parity), right
        elif number == 2:
            image, device = image_at(1 - z, x, parity), left
        else:
            image, device = image_at(z, x + 2, parity), across
        slot = (number - 1) * 2 + parity
        return remote(
            buf.at[image],
            buf.at[image],
            ag_send.at[which, slot],
            ag_recv.at[which, slot],
            device,
        )

    def gather_first(buf, which):
        for number, parity in ((6, 0), (7, 1), (4, 0), (6, 1), (7, 0), (4, 1)):
            gather_copy(buf, which, number, parity).start()

    def gather_second(buf, which):
        for parity, source in ((0, 6), (1, 7)):
            gather_copy(buf, which, source, parity).wait_recv()
            gather_copy(buf, which, 5, parity).start()
        gather_copy(buf, which, 4, 0).wait_recv()
        gather_copy(buf, which, 1, 0).start()
        gather_copy(buf, which, 2, 0).start()

    def gather_third(buf, which):
        gather_copy(buf, which, 4, 1).wait_recv()
        gather_copy(buf, which, 1, 1).start()
        gather_copy(buf, which, 2, 1).start()

    def gather_fourth(buf, which):
        for parity in (0, 1):
            gather_copy(buf, which, 5, parity).wait_recv()
            gather_copy(buf, which, 3, parity).start()

    def gather_last(buf, which):
        for number, parity in (
            (6, 1), (7, 0), (1, 0), (2, 0), (1, 1), (2, 1), (3, 0), (3, 1),
        ):
            gather_copy(buf, which, number, parity).wait_recv()
        for number in range(1, 8):
            for parity in (0, 1):
                gather_copy(buf, which, number, parity).wait_send()

    mine[0].wait()
    swaps[0].wait_recv()
    key_gain = gains_ref[1:2, :]

    def norm_keys(step, carry):
        parity = lax.div(step, subs)
        rows = columns(lax.rem(step, subs), TILE_TOK)
        entries = kraw[parity, rows, :].astype(F32)
        inverse = lax.rsqrt(jnp.mean(entries * entries, axis=-1, keepdims=True) + EPSILON)
        kbuf[chip + parity, rows, :] = (entries * inverse * key_gain).astype(BF16)
        return carry

    lax.fori_loop(0, 2 * subs, norm_keys, 0)
    gather_first(kbuf, 0)

    gcol[...] = jnp.transpose(jnp.broadcast_to(gains_ref[0:1, :], (HEAD_DIM, HEAD_DIM)))
    qgain[...] = jnp.zeros_like(qgain)
    for i in (2, 3):
        mine[i].wait()
        swaps[i].wait_recv()

    def prepare(t, carry):
        rows = columns(t, TEXT_TILE)
        gain_column = gcol[...]
        for h in range(group):
            cols = slice(h * HEAD_DIM, (h + 1) * HEAD_DIM)
            turned = jnp.transpose(q4[rows, cols].astype(F32))
            inverse = lax.rsqrt(jnp.mean(turned * turned, axis=0, keepdims=True) + EPSILON)
            unit = turned * inverse
            normed = unit * gain_column
            ut[t, :, cols] = unit
            rinv[t, :, cols] = inverse
            qnt[t, :, cols] = normed.astype(BF16)
            qn[t, cols, :] = jnp.transpose(normed).astype(BF16)
            cotangent = do4[rows, cols]
            don[t, cols, :] = cotangent
            dot_t[t, :, cols] = jnp.transpose(cotangent.astype(F32)).astype(BF16)

        @pl.when(t == 0)
        def _():
            gather_second(kbuf, 0)

        @pl.when(t == 1)
        def _():
            gather_third(kbuf, 0)

        @pl.when(t == 3)
        def _():
            gather_fourth(kbuf, 0)

        return carry

    lax.fori_loop(0, tile_total, prepare, 0)

    mine[1].wait()
    swaps[1].wait_recv()
    gather_first(vbuf, 1)
    gather_last(kbuf, 0)

    def forward(t, carry):
        slots = reads(t)
        keys = [kbuf[image] for image, _ in slots]
        for pair in range(pairs):
            cols = slice(pair * pair_width, (pair + 1) * pair_width)
            turned = qnt[t, :, cols]
            scratch = sbuf.at[pair % 2]
            peak = jnp.full((1, pair_width), -1e30, F32)
            for r, (_, length) in enumerate(slots):
                scores = dot(keys[r], turned)
                scratch[r * max_tokens : (r + 1) * max_tokens, :] = scores
                for s in range(subs):
                    top = jnp.max(scores[s * TILE_TOK : (s + 1) * TILE_TOK], axis=0, keepdims=True)
                    peak = jnp.maximum(peak, jnp.where(s * TILE_TOK < length, top, -1e30))
            total = jnp.zeros((1, pair_width), F32)
            for r, (_, length) in enumerate(slots):
                for s in range(subs):
                    begin = r * max_tokens + s * TILE_TOK
                    shift = jnp.where(s * TILE_TOK < length, peak, 1e30)
                    powers = jnp.exp2(
                        (scratch[begin : begin + TILE_TOK, :] - shift) * (scale * LOG2E)
                    )
                    scratch[begin : begin + TILE_TOK, :] = powers
                    total = total + jnp.sum(powers, axis=0, keepdims=True)
            inverse = 1.0 / total
            for r in range(READ_MOST * subs):
                begin = r * TILE_TOK
                wbuf[t, begin : begin + TILE_TOK, cols] = (
                    scratch[begin : begin + TILE_TOK, :] * inverse
                ).astype(BF16)
        cotangents = don[t]
        for r in range(READ_MOST):
            rows = slice(r * max_tokens, (r + 1) * max_tokens)
            vslot[t, r] = dot(wbuf[t, rows, :], cotangents)

        @pl.when(t == 1)
        def _():
            gather_second(vbuf, 1)

        @pl.when(t == 2)
        def _():
            gather_third(vbuf, 1)

        @pl.when(t == 3)
        def _():
            gather_fourth(vbuf, 1)

        return carry

    lax.fori_loop(0, tile_total, forward, 0)

    def sum_route(number, parity):
        if number == 1:
            return image_at(1 - z, x - 1, parity), left
        if number == 2:
            return image_at(1 - z, x + 1, parity), right
        if number == 3:
            return image_at(1 - z, x + 2, parity), across
        if number == 4:
            return image_at(1 - z, x, parity), across
        if number == 5:
            return image_at(z, x + 2, parity), (left, right)[parity]
        if number == 6:
            return image_at(z, x - 1, parity), left
        return image_at(z, x + 1, parity), right

    def sum_copy(send, land, which, number, parity):
        image, device = sum_route(number, parity)
        slot = (number - 1) * 2 + parity
        return remote(
            send.at[image], land.at[slot], rs_send.at[which, slot], rs_recv.at[which, slot], device
        )

    def share(slot_ref, image, s):
        rows = slice(s * TILE_TOK, (s + 1) * TILE_TOK)
        value = None
        for t in range(tile_total):
            place = image - first[t]
            weight = jnp.where((place >= 0) & (place < count[t]), 1.0, 0.0).astype(F32)
            part = slot_ref[t, jnp.clip(place, 0, READ_MOST - 1), rows, :] * weight
            value = part if value is None else value + part
        return value

    def summed(slot_ref, land, image, sources, s):
        value = share(slot_ref, image, s)
        for number, parity in sources:
            slot = (number - 1) * 2 + parity
            value = value + land[slot, s * TILE_TOK : (s + 1) * TILE_TOK, :].astype(F32)
        return value

    def send_sum(slot_ref, send, land, which, number, parity, sources):
        for source_number, source_parity in sources:
            sum_copy(send, land, which, source_number, source_parity).wait_recv()
        image, _ = sum_route(number, parity)
        for s in range(subs):
            rows = slice(s * TILE_TOK, (s + 1) * TILE_TOK)
            send[image, rows, :] = summed(slot_ref, land, image, sources, s).astype(BF16)
        sum_copy(send, land, which, number, parity).start()

    def sum_first(*refs):
        for parity in (0, 1):
            for number in (3, 1, 2):
                send_sum(*refs, number, parity, ())
        send_sum(*refs, 6, 1, ())
        send_sum(*refs, 7, 0, ())

    def sum_second(*refs):
        for parity in (0, 1):
            send_sum(*refs, 5, parity, ((3, parity),))
        for parity in (0, 1):
            send_sum(*refs, 4, parity, ((1, parity), (2, parity)))

    def sum_third(*refs):
        send_sum(*refs, 6, 0, ((5, 0),))
        send_sum(*refs, 7, 1, ((5, 1),))

    root_sources = (4, 6, 7)

    def sum_last(send, land, which):
        for number in root_sources:
            for parity in (0, 1):
                sum_copy(send, land, which, number, parity).wait_recv()
        for number in range(1, 8):
            for parity in (0, 1):
                sum_copy(send, land, which, number, parity).wait_send()

    value_refs = (vslot, vsend, vland, 0)
    key_refs = (kslot, ksend, kland, 1)
    sum_first(*value_refs)
    gather_last(vbuf, 1)

    def backward(t, carry):
        slots = reads(t)
        gain_column = gcol[...]
        gain_pair = jnp.concatenate([gain_column, gain_column], axis=1)
        values = [vbuf[image] for image, _ in slots]
        values_turned = [jnp.transpose(value) for value in values]
        keys_turned = [jnp.transpose(kbuf[image]) for image, _ in slots]
        rows_out = columns(t, TEXT_TILE)
        for pair in range(pairs):
            cols = slice(pair * pair_width, (pair + 1) * pair_width)
            cotangent = dot_t[t, :, cols]
            attended = None
            for r in range(READ_MOST):
                part = dot(
                    values_turned[r], wbuf[t, r * max_tokens : (r + 1) * max_tokens, cols]
                )
                attended = part if attended is None else attended + part
            row_dot = jnp.sum(attended * cotangent.astype(F32), axis=0, keepdims=True)
            grads = None
            for r in range(READ_MOST):
                rows = slice(r * max_tokens, (r + 1) * max_tokens)
                value_scores = dot(values[r], cotangent)
                score_grads = (
                    wbuf[t, rows, cols].astype(F32) * (value_scores - row_dot)
                ).astype(BF16)
                wbuf[t, rows, cols] = score_grads
                part = dot(keys_turned[r], score_grads)
                grads = part if grads is None else grads + part
            grads = grads * scale
            unit = ut[t, :, cols]
            scaled = grads * gain_pair
            mean = jnp.mean(scaled * unit, axis=0, keepdims=True)
            grad_query = rinv[t, :, cols] * (scaled - unit * mean)
            qgain[...] += grads * unit
            for h in range(2):
                head = slice(h * HEAD_DIM, (h + 1) * HEAD_DIM)
                out_cols = slice((2 * pair + h) * HEAD_DIM, (2 * pair + h + 1) * HEAD_DIM)
                obuf[rows_out, out_cols] = jnp.transpose(attended[:, head]).astype(BF16)
                dqbuf[rows_out, out_cols] = jnp.transpose(grad_query[:, head]).astype(BF16)
        normed = qn[t]
        for r in range(READ_MOST):
            rows = slice(r * max_tokens, (r + 1) * max_tokens)
            kslot[t, r] = dot(wbuf[t, rows, :], normed)

        @pl.when(t == 1)
        def _():
            sum_second(*value_refs)

        @pl.when(t == 2)
        def _():
            sum_third(*value_refs)

        return carry

    lax.fori_loop(0, tile_total, backward, 0)
    sum_first(*key_refs)

    out_cols = columns(core, half)
    head_cols = columns(core, HEAD_DIM)
    results = [
        (obuf.at[own_rows], obuf.at[other_rows], o_out, out_cols),
        (dqbuf.at[own_rows], dqbuf.at[other_rows], dq_out, out_cols),
        (gvbuf.at[core], gvbuf.at[other], dv_out, head_cols),
        (gkbuf.at[core], gkbuf.at[other], dk_out, head_cols),
    ]
    locals_out = [
        pltpu.make_async_copy(own, out.at[:, cols], out_local.at[i])
        for i, (own, _, out, cols) in enumerate(results)
    ]
    remotes_out = [
        remote(theirs, out.at[:, cols], out_send.at[i], out_recv.at[i], peer)
        for i, (_, theirs, out, cols) in enumerate(results)
    ]

    def put_out(i):
        locals_out[i].start()
        remotes_out[i].start()

    put_out(0)
    put_out(1)

    sum_last(vsend, vland, 0)
    for parity in (0, 1):
        sources = [(number, parity) for number in root_sources]
        for s in range(subs):
            rows = slice(s * TILE_TOK, (s + 1) * TILE_TOK)
            gvbuf[parity, rows, :] = summed(vslot, vland, chip + parity, sources, s).astype(BF16)
    put_out(2)

    sum_second(*key_refs)
    sum_third(*key_refs)
    sum_last(ksend, kland, 1)
    key_total = jnp.zeros((1, HEAD_DIM), F32)
    for parity in (0, 1):
        sources = [(number, parity) for number in root_sources]
        for s in range(subs):
            rows = slice(s * TILE_TOK, (s + 1) * TILE_TOK)
            grads = summed(kslot, kland, chip + parity, sources, s) * scale
            entries = kraw[parity, rows, :].astype(F32)
            inverse = lax.rsqrt(jnp.mean(entries * entries, axis=-1, keepdims=True) + EPSILON)
            unit = entries * inverse
            scaled = grads * key_gain
            mean = jnp.mean(scaled * unit, axis=-1, keepdims=True)
            gkbuf[parity, rows, :] = (inverse * (scaled - unit * mean)).astype(BF16)
            key_total = key_total + jnp.sum(grads * unit, axis=0, keepdims=True)
    put_out(3)
    query_total = jnp.sum(
        jnp.transpose(qgain[:, :HEAD_DIM] + qgain[:, HEAD_DIM:]), axis=0, keepdims=True
    )
    gain_out[...] = jnp.concatenate([query_total, key_total], axis=0)

    for copy in swaps:
        copy.wait_send()
    for i in range(len(results)):
        locals_out[i].wait()
        remotes_out[i].wait_send()
        remotes_out[i].wait_recv()


def on_device(queries, image_keys, image_values, norm_gains, image_tiles, read_mask, grad_attended):
    tokens, width = queries.shape[1:]
    max_tokens, kv_width = image_keys.shape[2:]
    group = width // kv_width
    images = read_mask.shape[2]
    half = group * HEAD_DIM
    tile_total = 2 * tokens // TEXT_TILE
    slot_width = READ_MOST * max_tokens
    hbm = pl.BlockSpec(memory_space=pl.ANY)
    vmem = pl.BlockSpec(memory_space=pltpu.VMEM)
    smem = pl.BlockSpec(memory_space=pltpu.SMEM)
    dma = pltpu.SemaphoreType.DMA
    block = (images, max_tokens, HEAD_DIM)
    slots = (tile_total, READ_MOST, max_tokens, HEAD_DIM)
    turned = (tile_total, HEAD_DIM, half)
    plain = (tile_total, half, HEAD_DIM)
    scratch = [
        pltpu.VMEM((2 * tokens, half), BF16),
        pltpu.VMEM((2 * tokens, half), BF16),
        pltpu.VMEM((2, max_tokens, HEAD_DIM), BF16),
        pltpu.VMEM(block, BF16),
        pltpu.VMEM(block, BF16),
        pltpu.VMEM(plain, BF16),
        pltpu.VMEM(turned, BF16),
        pltpu.VMEM(turned, BF16),
        pltpu.VMEM(plain, BF16),
        pltpu.VMEM(turned, F32),
        pltpu.VMEM((tile_total, 1, half), F32),
        pltpu.VMEM((tile_total, slot_width, half), BF16),
        pltpu.VMEM((2, slot_width, 2 * HEAD_DIM), F32),
        pltpu.VMEM(slots, F32),
        pltpu.VMEM(slots, F32),
        pltpu.VMEM(block, BF16),
        pltpu.VMEM(block, BF16),
        pltpu.VMEM((14, max_tokens, HEAD_DIM), BF16),
        pltpu.VMEM((14, max_tokens, HEAD_DIM), BF16),
        pltpu.VMEM((2 * tokens, half), BF16),
        pltpu.VMEM((2 * tokens, half), BF16),
        pltpu.VMEM((2, max_tokens, HEAD_DIM), BF16),
        pltpu.VMEM((2, max_tokens, HEAD_DIM), BF16),
        pltpu.VMEM((HEAD_DIM, 2 * HEAD_DIM), F32),
        pltpu.VMEM((HEAD_DIM, HEAD_DIM), F32),
        dma((4,)),
        dma((4,)),
        dma((4,)),
        dma((2, 14)),
        dma((2, 14)),
        dma((2, 14)),
        dma((2, 14)),
        dma((4,)),
        dma((4,)),
        dma((4,)),
    ]
    attended, grad_queries, grad_keys, grad_values, gain_parts = pl.pallas_call(
        functools.partial(kernel, images, group),
        out_shape=[
            jax.ShapeDtypeStruct((tokens, width), BF16),
            jax.ShapeDtypeStruct((tokens, width), BF16),
            jax.ShapeDtypeStruct((max_tokens, kv_width), BF16),
            jax.ShapeDtypeStruct((max_tokens, kv_width), BF16),
            jax.ShapeDtypeStruct((2, HEAD_DIM), F32),
        ],
        in_specs=[hbm, hbm, hbm, hbm, vmem, smem, smem],
        out_specs=[hbm, hbm, hbm, hbm, vmem],
        scratch_shapes=scratch,
        compiler_params=pltpu.CompilerParams(
            collective_id=0, has_side_effects=True, vmem_limit_bytes=60 * 1024 * 1024
        ),
    )(
        queries[0],
        grad_attended[0],
        image_keys[0, 0],
        image_values[0, 0],
        norm_gains,
        image_tiles[0],
        read_mask[0],
    )
    grad_gains = lax.psum(gain_parts, ("dp", "seq", "mp"))
    return (
        attended[None],
        grad_queries[None],
        grad_keys[None, None],
        grad_values[None, None],
        grad_gains,
    )


def solution(mesh):
    in_specs = (
        P("dp", "seq", "mp"),
        P("dp", "seq", None, "mp"),
        P("dp", "seq", None, "mp"),
        P(),
        P("dp", None),
        P("dp", None, None),
        P("dp", "seq", "mp"),
    )
    out_specs = (
        P("dp", "seq", "mp"),
        P("dp", "seq", "mp"),
        P("dp", "seq", None, "mp"),
        P("dp", "seq", None, "mp"),
        P(),
    )
    return jax.shard_map(
        on_device, mesh=mesh, in_specs=in_specs, out_specs=out_specs, check_vma=False
    )
```

```python
import functools

import jax
import jax.numpy as jnp
from jax import lax
from jax.experimental import pallas as pl
from jax.experimental.pallas import tpu as pltpu
from jax.sharding import PartitionSpec as P

HEAD_DIM = 128
TEXT_TILE = 128
TILE_TOK = 128
READ_MOST = 3
EPSILON = 1e-05
LOG2E = 1.4426950408889634
MESH = pl.DeviceIdType.MESH
BF16 = jnp.bfloat16
F32 = jnp.float32

RING = 4


def dot(a, b):
    return jnp.dot(a, b, preferred_element_type=F32)


def kernel(
    images,
    group,
    dp_total,
    mp_total,
    q_ref,
    do_ref,
    k_ref,
    v_ref,
    gains_ref,
    tiles_ref,
    mask_ref,
    o_out,
    dq_out,
    dk_out,
    dv_out,
    gain_out,
    q4,
    do4,
    kraw,
    kbuf,
    vbuf,
    qn,
    qnt,
    dot_t,
    don,
    ut,
    rinv,
    wbuf,
    sbuf,
    vslot,
    kslot,
    vsend,
    ksend,
    vland,
    kland,
    obuf,
    dqbuf,
    gkbuf,
    gvbuf,
    oturn,
    overlap,
    gcol,
    zgain,
    ygain,
    cgain,
    xgain,
    local_sem,
    swap_send,
    swap_recv,
    ag_send,
    ag_recv,
    rs_send,
    rs_recv,
    out_local,
    out_send,
    out_recv,
    zsend,
    zrecv,
    ysend,
    yrecv,
    csend,
    crecv,
    xsend,
    xrecv,
):
    max_tokens = k_ref.shape[0]
    tokens = q_ref.shape[0]
    half = group * HEAD_DIM
    pair_width = 2 * HEAD_DIM
    pairs = group // 2
    tile_total = 2 * tokens // TEXT_TILE
    subs = max_tokens // TILE_TOK
    scale = HEAD_DIM ** (-0.5)

    seq = lax.axis_index("seq")
    core = lax.rem(seq, 2)
    x = lax.rem(lax.div(seq, 2), RING)
    z = lax.div(seq, 2 * RING)
    other = 1 - core

    def image_at(zz, xx, parity):
        return zz * (2 * RING) + lax.rem(xx + RING, RING) * 2 + parity

    peer = image_at(z, x, other)
    dp = lax.axis_index("dp")
    mp = lax.axis_index("mp")
    right = image_at(z, x + 1, core)
    left = image_at(z, x - 1, core)
    across = image_at(1 - z, x, core)
    chip = image_at(z, x, 0)

    def columns(index, width):
        return pl.ds(pl.multiple_of(index * width, width), width)

    own_rows = columns(core, tokens)
    other_rows = columns(other, tokens)

    def remote(src, dst, send_sem, recv_sem, device):
        device = device if isinstance(device, dict) else {"seq": device}
        return pltpu.make_async_remote_copy(
            src_ref=src,
            dst_ref=dst,
            send_sem=send_sem,
            recv_sem=recv_sem,
            device_id=device,
            device_id_type=MESH,
        )

    mine = [
        pltpu.make_async_copy(k_ref.at[:, columns(core, HEAD_DIM)], kraw.at[core], local_sem.at[0]),
        pltpu.make_async_copy(
            v_ref.at[:, columns(core, HEAD_DIM)], vbuf.at[chip + core], local_sem.at[1]
        ),
        pltpu.make_async_copy(q_ref.at[:, columns(core, half)], q4.at[own_rows], local_sem.at[2]),
        pltpu.make_async_copy(do_ref.at[:, columns(core, half)], do4.at[own_rows], local_sem.at[3]),
    ]
    for copy in mine:
        copy.start()

    barrier = pltpu.get_barrier_semaphore()
    chain = 2 * mp_total

    def z_device(k):
        place = lax.rem(2 * mp + z + k, chain)
        return {"seq": image_at(lax.rem(place, 2), x, core), "mp": lax.div(place, 2)}

    def y_device(k):
        return {"dp": lax.rem(dp + k, dp_total)}

    def x_device(k):
        return {"seq": image_at(z, x + k, core)}

    greeted = [{"seq": peer}]
    greeted += [x_device(k) for k in range(1, RING)]
    greeted += [y_device(k) for k in range(1, dp_total)]
    greeted += [z_device(k) for k in range(1, chain)]
    for device in greeted:
        pl.semaphore_signal(barrier, inc=1, device_id=device, device_id_type=MESH)
    pl.semaphore_wait(barrier, len(greeted))

    swaps = [
        (k_ref.at[:, columns(other, HEAD_DIM)], kraw.at[core]),
        (v_ref.at[:, columns(other, HEAD_DIM)], vbuf.at[chip + core]),
        (q_ref.at[:, columns(other, half)], q4.at[own_rows]),
        (do_ref.at[:, columns(other, half)], do4.at[own_rows]),
    ]
    swaps = [
        remote(src, dst, swap_send.at[i], swap_recv.at[i], peer)
        for i, (src, dst) in enumerate(swaps)
    ]
    for copy in swaps:
        copy.start()

    tile_base = lax.div(seq, 2) * tile_total
    first, count = [], []
    for t in range(tile_total):
        begin = jnp.int32(images)
        total = jnp.int32(0)
        for i in range(images):
            flag = mask_ref[i, tile_base + t]
            total = total + flag
            begin = jnp.where((flag == 1) & (begin == images), i, begin)
        first.append(begin)
        count.append(total)

    def pick(values, t):
        out = values[0]
        for k in range(1, len(values)):
            out = jnp.where(t == k, values[k], out)
        return out

    def reads(t):
        begin = pick(first, t)
        total = pick(count, t)
        found = []
        for r in range(READ_MOST):
            image = jnp.minimum(begin + r, images - 1)
            length = jnp.where(r < total, tiles_ref[image] * TILE_TOK, 0)
            found.append((image, length))
        return found

    def gather_copy(buf, which, number, parity):
        if number == 6:
            image, device = image_at(z, x, parity), right
        elif number == 7:
            image, device = image_at(z, x, parity), left
        elif number == 4:
            image, device = image_at(z, x, parity), across
        elif number == 5 and parity == 0:
            image, device = image_at(z, x - 1, 0), right
        elif number == 5:
            image, device = image_at(z, x + 1, 1), left
        elif number == 1:
            image, device = image_at(1 - z, x, parity), right
        elif number == 2:
            image, device = image_at(1 - z, x, parity), left
        else:
            image, device = image_at(z, x + 2, parity), across
        slot = (number - 1) * 2 + parity
        return remote(
            buf.at[image],
            buf.at[image],
            ag_send.at[which, slot],
            ag_recv.at[which, slot],
            device,
        )

    def gather_first(buf, which):
        for number, parity in ((6, 0), (7, 1), (4, 0), (6, 1), (7, 0), (4, 1)):
            gather_copy(buf, which, number, parity).start()

    def gather_second(buf, which):
        for parity, source in ((0, 6), (1, 7)):
            gather_copy(buf, which, source, parity).wait_recv()
            gather_copy(buf, which, 5, parity).start()
        gather_copy(buf, which, 4, 0).wait_recv()
        gather_copy(buf, which, 1, 0).start()
        gather_copy(buf, which, 2, 0).start()

    def gather_third(buf, which):
        gather_copy(buf, which, 4, 1).wait_recv()
        gather_copy(buf, which, 1, 1).start()
        gather_copy(buf, which, 2, 1).start()

    def gather_fourth(buf, which):
        for parity in (0, 1):
            gather_copy(buf, which, 5, parity).wait_recv()
            gather_copy(buf, which, 3, parity).start()

    def gather_last(buf, which):
        for number, parity in (
            (6, 1), (7, 0), (1, 0), (2, 0), (1, 1), (2, 1), (3, 0), (3, 1),
        ):
            gather_copy(buf, which, number, parity).wait_recv()
        for number in range(1, 8):
            for parity in (0, 1):
                gather_copy(buf, which, number, parity).wait_send()

    mine[0].wait()
    swaps[0].wait_recv()
    key_gain = gains_ref[1:2, :]

    def norm_keys(step, carry):
        parity = lax.div(step, subs)
        rows = columns(lax.rem(step, subs), TILE_TOK)
        entries = kraw[parity, rows, :].astype(F32)
        inverse = lax.rsqrt(jnp.mean(entries * entries, axis=-1, keepdims=True) + EPSILON)
        kbuf[chip + parity, rows, :] = (entries * inverse * key_gain).astype(BF16)
        return carry

    lax.fori_loop(0, 2 * subs, norm_keys, 0)
    gather_first(kbuf, 0)

    gcol[...] = jnp.transpose(jnp.broadcast_to(gains_ref[0:1, :], (HEAD_DIM, HEAD_DIM)))
    overlap[...] = jnp.zeros_like(overlap)
    for i in (2, 3):
        mine[i].wait()
        swaps[i].wait_recv()

    def prepare(t, carry):
        rows = columns(t, TEXT_TILE)
        gain_column = gcol[...]
        for h in range(group):
            cols = slice(h * HEAD_DIM, (h + 1) * HEAD_DIM)
            turned = jnp.transpose(q4[rows, cols].astype(F32))
            inverse = lax.rsqrt(jnp.mean(turned * turned, axis=0, keepdims=True) + EPSILON)
            unit = turned * inverse
            normed = unit * gain_column
            ut[t, :, cols] = unit
            rinv[t, :, cols] = inverse
            qnt[t, :, cols] = normed.astype(BF16)
            qn[t, cols, :] = jnp.transpose(normed).astype(BF16)
            cotangent = do4[rows, cols]
            don[t, cols, :] = cotangent
            dot_t[t, :, cols] = jnp.transpose(cotangent.astype(F32)).astype(BF16)

        return carry

    lax.fori_loop(0, tile_total, prepare, 0)
    gather_second(kbuf, 0)
    gather_third(kbuf, 0)
    gather_fourth(kbuf, 0)

    mine[1].wait()
    swaps[1].wait_recv()
    gather_first(vbuf, 1)
    gather_last(kbuf, 0)

    def forward(t, carry):
        slots = reads(t)
        keys = [kbuf[image] for image, _ in slots]
        for pair in range(pairs):
            cols = slice(pair * pair_width, (pair + 1) * pair_width)
            turned = qnt[t, :, cols]
            scratch = sbuf.at[pair % 2]
            peak = jnp.full((1, pair_width), -1e30, F32)
            for r, (_, length) in enumerate(slots):
                scores = dot(keys[r], turned)
                scratch[r * max_tokens : (r + 1) * max_tokens, :] = scores
                for s in range(subs):
                    top = jnp.max(scores[s * TILE_TOK : (s + 1) * TILE_TOK], axis=0, keepdims=True)
                    peak = jnp.maximum(peak, jnp.where(s * TILE_TOK < length, top, -1e30))
            total = jnp.zeros((1, pair_width), F32)
            for r, (_, length) in enumerate(slots):
                for s in range(subs):
                    begin = r * max_tokens + s * TILE_TOK
                    shift = jnp.where(s * TILE_TOK < length, peak, 1e30)
                    powers = jnp.exp2(
                        (scratch[begin : begin + TILE_TOK, :] - shift) * (scale * LOG2E)
                    )
                    scratch[begin : begin + TILE_TOK, :] = powers
                    total = total + jnp.sum(powers, axis=0, keepdims=True)
            inverse = 1.0 / total
            for r in range(READ_MOST * subs):
                begin = r * TILE_TOK
                wbuf[t, begin : begin + TILE_TOK, cols] = (
                    scratch[begin : begin + TILE_TOK, :] * inverse
                ).astype(BF16)
        cotangents = don[t]
        for r in range(READ_MOST):
            rows = slice(r * max_tokens, (r + 1) * max_tokens)
            vslot[t, r] = dot(wbuf[t, rows, :], cotangents)

        @pl.when(t == 0)
        def _():
            gather_second(vbuf, 1)

        @pl.when(t == 1)
        def _():
            gather_third(vbuf, 1)

        @pl.when(t == 2)
        def _():
            gather_fourth(vbuf, 1)

        return carry

    lax.fori_loop(0, tile_total, forward, 0)

    def sum_route(number, parity):
        if number == 1:
            return image_at(1 - z, x - 1, parity), left
        if number == 2:
            return image_at(1 - z, x + 1, parity), right
        if number == 3:
            return image_at(1 - z, x + 2, parity), across
        if number == 4:
            return image_at(1 - z, x, parity), across
        if number == 5:
            return image_at(z, x + 2, parity), (left, right)[parity]
        if number == 6:
            return image_at(z, x - 1, parity), left
        return image_at(z, x + 1, parity), right

    def sum_copy(send, land, which, number, parity):
        image, device = sum_route(number, parity)
        slot = (number - 1) * 2 + parity
        return remote(
            send.at[image], land.at[slot], rs_send.at[which, slot], rs_recv.at[which, slot], device
        )

    def share(slot_ref, image, s):
        rows = slice(s * TILE_TOK, (s + 1) * TILE_TOK)
        value = None
        for t in range(tile_total):
            place = image - first[t]
            weight = jnp.where((place >= 0) & (place < count[t]), 1.0, 0.0).astype(F32)
            part = slot_ref[t, jnp.clip(place, 0, READ_MOST - 1), rows, :] * weight
            value = part if value is None else value + part
        return value

    def summed(slot_ref, land, image, sources, s):
        value = share(slot_ref, image, s)
        for number, parity in sources:
            slot = (number - 1) * 2 + parity
            value = value + land[slot, s * TILE_TOK : (s + 1) * TILE_TOK, :].astype(F32)
        return value

    def send_sum(slot_ref, send, land, which, number, parity, sources):
        for source_number, source_parity in sources:
            sum_copy(send, land, which, source_number, source_parity).wait_recv()
        image, _ = sum_route(number, parity)
        for s in range(subs):
            rows = slice(s * TILE_TOK, (s + 1) * TILE_TOK)
            send[image, rows, :] = summed(slot_ref, land, image, sources, s).astype(BF16)
        sum_copy(send, land, which, number, parity).start()

    def sum_first(*refs):
        for parity in (0, 1):
            for number in (3, 1, 2):
                send_sum(*refs, number, parity, ())
        send_sum(*refs, 6, 1, ())
        send_sum(*refs, 7, 0, ())

    def sum_second(*refs):
        for parity in (0, 1):
            send_sum(*refs, 5, parity, ((3, parity),))
        for parity in (0, 1):
            send_sum(*refs, 4, parity, ((1, parity), (2, parity)))

    def sum_third(*refs):
        send_sum(*refs, 6, 0, ((5, 0),))
        send_sum(*refs, 7, 1, ((5, 1),))

    root_sources = (4, 6, 7)

    def sum_last(send, land, which):
        for number in root_sources:
            for parity in (0, 1):
                sum_copy(send, land, which, number, parity).wait_recv()
        for number in range(1, 8):
            for parity in (0, 1):
                sum_copy(send, land, which, number, parity).wait_send()

    value_refs = (vslot, vsend, vland, 0)
    key_refs = (kslot, ksend, kland, 1)
    sum_first(*value_refs)
    gather_last(vbuf, 1)

    def backward(t, carry):
        slots = reads(t)
        values = [vbuf[image] for image, _ in slots]
        values_turned = [jnp.transpose(value) for value in values]
        for pair in range(pairs):
            cols = slice(pair * pair_width, (pair + 1) * pair_width)
            cotangent = dot_t[t, :, cols]
            attended = None
            for r in range(READ_MOST):
                part = dot(
                    values_turned[r], wbuf[t, r * max_tokens : (r + 1) * max_tokens, cols]
                )
                attended = part if attended is None else attended + part
            oturn[t, :, cols] = attended.astype(BF16)
            row_dot = jnp.sum(attended * cotangent.astype(F32), axis=0, keepdims=True)
            for r in range(READ_MOST):
                rows = slice(r * max_tokens, (r + 1) * max_tokens)
                value_scores = dot(values[r], cotangent)
                wbuf[t, rows, cols] = (
                    wbuf[t, rows, cols].astype(F32) * (value_scores - row_dot)
                ).astype(BF16)
        normed = qn[t]
        for r, (image, _) in enumerate(slots):
            rows = slice(r * max_tokens, (r + 1) * max_tokens)
            part = dot(wbuf[t, rows, :], normed)
            kslot[t, r] = part
            product = part * kbuf[image].astype(F32)
            overlap[...] += jnp.sum(product.reshape(max_tokens // 8, 8, HEAD_DIM), axis=0)

        @pl.when(t == 2)
        def _():
            sum_second(*value_refs)

        return carry

    lax.fori_loop(0, tile_total, backward, 0)

    def gain_copy(buf, send, recv, place, k, device):
        return remote(buf.at[place], buf.at[place], send.at[k - 1], recv.at[place], device)

    def gain_start(buf, send, recv, place, total, device_of, value):
        buf[place] = value
        for k in range(1, total):
            gain_copy(buf, send, recv, place, k, device_of(k)).start()

    def gain_finish(buf, send, recv, place, total, device_of):
        for k in range(1, total):
            source = lax.rem(place + k, total)
            gain_copy(buf, send, recv, source, k, device_of(k)).wait_recv()
        for k in range(1, total):
            gain_copy(buf, send, recv, place, k, device_of(k)).wait_send()
        value = buf[0]
        for k in range(1, total):
            value = value + buf[k]
        return value

    z_stage = (zgain, zsend, zrecv, 2 * mp + z, chain, z_device)
    y_stage = (ygain, ysend, yrecv, dp, dp_total, y_device)
    core_stage = (cgain, csend, crecv, core, 2, lambda k: {"seq": peer})
    x_stage = (xgain, xsend, xrecv, x, RING, x_device)

    gain_start(*z_stage, overlap[...])
    sum_first(*key_refs)
    sum_third(*value_refs)

    def queries_backward(t, carry):
        slots = reads(t)
        gain_column = gcol[...]
        gain_pair = jnp.concatenate([gain_column, gain_column], axis=1)
        keys_turned = [jnp.transpose(kbuf[image]) for image, _ in slots]
        rows_out = columns(t, TEXT_TILE)
        for pair in range(pairs):
            cols = slice(pair * pair_width, (pair + 1) * pair_width)
            grads = None
            for r in range(READ_MOST):
                part = dot(keys_turned[r], wbuf[t, r * max_tokens : (r + 1) * max_tokens, cols])
                grads = part if grads is None else grads + part
            grads = grads * scale
            unit = ut[t, :, cols]
            scaled = grads * gain_pair
            mean = jnp.mean(scaled * unit, axis=0, keepdims=True)
            grad_query = rinv[t, :, cols] * (scaled - unit * mean)
            for h in range(2):
                head = slice(h * HEAD_DIM, (h + 1) * HEAD_DIM)
                out_cols = slice((2 * pair + h) * HEAD_DIM, (2 * pair + h + 1) * HEAD_DIM)
                obuf[rows_out, out_cols] = jnp.transpose(oturn[t, :, out_cols])
                dqbuf[rows_out, out_cols] = jnp.transpose(grad_query[:, head]).astype(BF16)

        @pl.when(t == 0)
        def _():
            gain_start(*y_stage, gain_finish(*z_stage))

        @pl.when(t == 1)
        def _():
            gain_start(*core_stage, gain_finish(*y_stage))

        @pl.when(t == 2)
        def _():
            gain_start(*x_stage, gain_finish(*core_stage))
            sum_second(*key_refs)

        return carry

    lax.fori_loop(0, tile_total, queries_backward, 0)

    out_cols = columns(core, half)
    head_cols = columns(core, HEAD_DIM)
    results = [
        (obuf.at[own_rows], obuf.at[other_rows], o_out, out_cols),
        (dqbuf.at[own_rows], dqbuf.at[other_rows], dq_out, out_cols),
        (gvbuf.at[core], gvbuf.at[other], dv_out, head_cols),
        (gkbuf.at[core], gkbuf.at[other], dk_out, head_cols),
    ]
    locals_out = [
        pltpu.make_async_copy(own, out.at[:, cols], out_local.at[i])
        for i, (own, _, out, cols) in enumerate(results)
    ]
    remotes_out = [
        remote(theirs, out.at[:, cols], out_send.at[i], out_recv.at[i], peer)
        for i, (_, theirs, out, cols) in enumerate(results)
    ]

    def put_out(i):
        locals_out[i].start()
        remotes_out[i].start()

    put_out(0)
    put_out(1)

    sum_last(vsend, vland, 0)
    for parity in (0, 1):
        sources = [(number, parity) for number in root_sources]
        for s in range(subs):
            rows = slice(s * TILE_TOK, (s + 1) * TILE_TOK)
            gvbuf[parity, rows, :] = summed(vslot, vland, chip + parity, sources, s).astype(BF16)
    put_out(2)

    sum_third(*key_refs)
    sum_last(ksend, kland, 1)
    for parity in (0, 1):
        sources = [(number, parity) for number in root_sources]
        for s in range(subs):
            rows = slice(s * TILE_TOK, (s + 1) * TILE_TOK)
            grads = summed(kslot, kland, chip + parity, sources, s) * scale
            entries = kraw[parity, rows, :].astype(F32)
            inverse = lax.rsqrt(jnp.mean(entries * entries, axis=-1, keepdims=True) + EPSILON)
            unit = entries * inverse
            scaled = grads * key_gain
            mean = jnp.mean(scaled * unit, axis=-1, keepdims=True)
            gkbuf[parity, rows, :] = (inverse * (scaled - unit * mean)).astype(BF16)
    put_out(3)
    products = jnp.sum(gain_finish(*x_stage), axis=0, keepdims=True) * scale
    gain_out[...] = products / gains_ref[...]

    for copy in swaps:
        copy.wait_send()
    for i in range(len(results)):
        locals_out[i].wait()
        remotes_out[i].wait_send()
        remotes_out[i].wait_recv()


def on_device(
    dp_total,
    mp_total,
    queries,
    image_keys,
    image_values,
    norm_gains,
    image_tiles,
    read_mask,
    grad_attended,
):
    tokens, width = queries.shape[1:]
    max_tokens, kv_width = image_keys.shape[2:]
    group = width // kv_width
    images = read_mask.shape[2]
    half = group * HEAD_DIM
    tile_total = 2 * tokens // TEXT_TILE
    slot_width = READ_MOST * max_tokens
    hbm = pl.BlockSpec(memory_space=pl.ANY)
    vmem = pl.BlockSpec(memory_space=pltpu.VMEM)
    smem = pl.BlockSpec(memory_space=pltpu.SMEM)
    dma = pltpu.SemaphoreType.DMA
    block = (images, max_tokens, HEAD_DIM)
    slots = (tile_total, READ_MOST, max_tokens, HEAD_DIM)
    turned = (tile_total, HEAD_DIM, half)
    plain = (tile_total, half, HEAD_DIM)
    scratch = [
        pltpu.VMEM((2 * tokens, half), BF16),
        pltpu.VMEM((2 * tokens, half), BF16),
        pltpu.VMEM((2, max_tokens, HEAD_DIM), BF16),
        pltpu.VMEM(block, BF16),
        pltpu.VMEM(block, BF16),
        pltpu.VMEM(plain, BF16),
        pltpu.VMEM(turned, BF16),
        pltpu.VMEM(turned, BF16),
        pltpu.VMEM(plain, BF16),
        pltpu.VMEM(turned, F32),
        pltpu.VMEM((tile_total, 1, half), F32),
        pltpu.VMEM((tile_total, slot_width, half), BF16),
        pltpu.VMEM((2, slot_width, 2 * HEAD_DIM), F32),
        pltpu.VMEM(slots, F32),
        pltpu.VMEM(slots, F32),
        pltpu.VMEM(block, BF16),
        pltpu.VMEM(block, BF16),
        pltpu.VMEM((14, max_tokens, HEAD_DIM), BF16),
        pltpu.VMEM((14, max_tokens, HEAD_DIM), BF16),
        pltpu.VMEM((2 * tokens, half), BF16),
        pltpu.VMEM((2 * tokens, half), BF16),
        pltpu.VMEM((2, max_tokens, HEAD_DIM), BF16),
        pltpu.VMEM((2, max_tokens, HEAD_DIM), BF16),
        pltpu.VMEM(turned, BF16),
        pltpu.VMEM((8, HEAD_DIM), F32),
        pltpu.VMEM((HEAD_DIM, HEAD_DIM), F32),
        pltpu.VMEM((2 * mp_total, 8, HEAD_DIM), F32),
        pltpu.VMEM((dp_total, 8, HEAD_DIM), F32),
        pltpu.VMEM((2, 8, HEAD_DIM), F32),
        pltpu.VMEM((RING, 8, HEAD_DIM), F32),
        dma((4,)),
        dma((4,)),
        dma((4,)),
        dma((2, 14)),
        dma((2, 14)),
        dma((2, 14)),
        dma((2, 14)),
        dma((4,)),
        dma((4,)),
        dma((4,)),
        dma((2 * mp_total,)),
        dma((2 * mp_total,)),
        dma((dp_total,)),
        dma((dp_total,)),
        dma((2,)),
        dma((2,)),
        dma((RING,)),
        dma((RING,)),
    ]
    attended, grad_queries, grad_keys, grad_values, grad_gains = pl.pallas_call(
        functools.partial(kernel, images, group, dp_total, mp_total),
        out_shape=[
            jax.ShapeDtypeStruct((tokens, width), BF16),
            jax.ShapeDtypeStruct((tokens, width), BF16),
            jax.ShapeDtypeStruct((max_tokens, kv_width), BF16),
            jax.ShapeDtypeStruct((max_tokens, kv_width), BF16),
            jax.ShapeDtypeStruct((2, HEAD_DIM), F32),
        ],
        in_specs=[hbm, hbm, hbm, hbm, vmem, smem, smem],
        out_specs=[hbm, hbm, hbm, hbm, vmem],
        scratch_shapes=scratch,
        compiler_params=pltpu.CompilerParams(
            collective_id=0, has_side_effects=True, vmem_limit_bytes=60 * 1024 * 1024
        ),
    )(
        queries[0],
        grad_attended[0],
        image_keys[0, 0],
        image_values[0, 0],
        norm_gains,
        image_tiles[0],
        jnp.transpose(read_mask[0]),
    )
    return (
        attended[None],
        grad_queries[None],
        grad_keys[None, None],
        grad_values[None, None],
        grad_gains,
    )


def solution(mesh):
    in_specs = (
        P("dp", "seq", "mp"),
        P("dp", "seq", None, "mp"),
        P("dp", "seq", None, "mp"),
        P(),
        P("dp", None),
        P("dp", None, None),
        P("dp", "seq", "mp"),
    )
    out_specs = (
        P("dp", "seq", "mp"),
        P("dp", "seq", "mp"),
        P("dp", "seq", None, "mp"),
        P("dp", "seq", None, "mp"),
        P(),
    )
    per_device = functools.partial(on_device, mesh.shape["dp"], mesh.shape["mp"])
    return jax.shard_map(
        per_device, mesh=mesh, in_specs=in_specs, out_specs=out_specs, check_vma=False
    )
```

```python
import functools

import jax
import jax.numpy as jnp
from jax import lax
from jax.experimental import pallas as pl
from jax.experimental.pallas import tpu as pltpu
from jax.sharding import PartitionSpec as P

HEAD_DIM = 128
TEXT_TILE = 128
TILE_TOK = 128
READ_MOST = 3
EPSILON = 1e-05
LOG2E = 1.4426950408889634
MESH = pl.DeviceIdType.MESH
BF16 = jnp.bfloat16
MOVE_CUTS = 4
F32 = jnp.float32

RING = 4


def dot(a, b):
    return jnp.dot(a, b, preferred_element_type=F32)


def kernel(
    images,
    group,
    dp_total,
    mp_total,
    q_ref,
    do_ref,
    k_ref,
    v_ref,
    gains_ref,
    tiles_ref,
    mask_ref,
    o_out,
    dq_out,
    dk_out,
    dv_out,
    gain_out,
    q4,
    do4,
    kraw,
    kbuf,
    vbuf,
    qn,
    qnt,
    dot_t,
    don,
    ut,
    rinv,
    wbuf,
    sbuf,
    vslot,
    kslot,
    vsend,
    ksend,
    vland,
    kland,
    obuf,
    dqbuf,
    gkbuf,
    gvbuf,
    early,
    unit_keys,
    inverse_keys,
    oturn,
    overlap,
    gcol,
    zgain,
    ygain,
    cgain,
    xgain,
    local_sem,
    swap_send,
    swap_recv,
    ag_send,
    ag_recv,
    rs_send,
    rs_recv,
    out_local,
    out_send,
    out_recv,
    zsend,
    zrecv,
    ysend,
    yrecv,
    csend,
    crecv,
    xsend,
    xrecv,
):
    max_tokens = k_ref.shape[0]
    tokens = q_ref.shape[0]
    half = group * HEAD_DIM
    pair_width = 2 * HEAD_DIM
    pairs = group // 2
    tile_total = 2 * tokens // TEXT_TILE
    subs = max_tokens // TILE_TOK
    scale = HEAD_DIM ** (-0.5)

    seq = lax.axis_index("seq")
    core = lax.rem(seq, 2)
    x = lax.rem(lax.div(seq, 2), RING)
    z = lax.div(seq, 2 * RING)
    other = 1 - core

    def image_at(zz, xx, parity):
        return zz * (2 * RING) + lax.rem(xx + RING, RING) * 2 + parity

    peer = image_at(z, x, other)
    dp = lax.axis_index("dp")
    mp = lax.axis_index("mp")
    right = image_at(z, x + 1, core)
    left = image_at(z, x - 1, core)
    across = image_at(1 - z, x, core)
    chip = image_at(z, x, 0)

    def columns(index, width):
        return pl.ds(pl.multiple_of(index * width, width), width)

    own_rows = columns(core, tokens)
    other_rows = columns(other, tokens)

    def remote(src, dst, send_sem, recv_sem, device):
        device = device if isinstance(device, dict) else {"seq": device}
        return pltpu.make_async_remote_copy(
            src_ref=src,
            dst_ref=dst,
            send_sem=send_sem,
            recv_sem=recv_sem,
            device_id=device,
            device_id_type=MESH,
        )

    barrier = pltpu.get_barrier_semaphore()
    chain = 2 * mp_total

    def z_device(k):
        place = lax.rem(2 * mp + z + k, chain)
        return {"seq": image_at(lax.rem(place, 2), x, core), "mp": lax.div(place, 2)}

    def y_device(k):
        return {"dp": lax.rem(dp + k, dp_total)}

    def x_device(k):
        return {"seq": image_at(z, x + k, core)}

    greeted = [{"seq": peer}]
    greeted += [x_device(k) for k in range(1, RING)]
    greeted += [y_device(k) for k in range(1, dp_total)]
    greeted += [z_device(k) for k in range(1, chain)]
    for device in greeted:
        pl.semaphore_signal(barrier, inc=1, device_id=device, device_id_type=MESH)

    mine = [
        pltpu.make_async_copy(k_ref.at[:, columns(core, HEAD_DIM)], kraw.at[core], local_sem.at[0]),
        pltpu.make_async_copy(
            v_ref.at[:, columns(core, HEAD_DIM)], vbuf.at[chip + core], local_sem.at[1]
        ),
        pltpu.make_async_copy(q_ref.at[:, columns(core, half)], q4.at[own_rows], local_sem.at[2]),
        pltpu.make_async_copy(do_ref.at[:, columns(core, half)], do4.at[own_rows], local_sem.at[3]),
    ]
    for copy in mine:
        copy.start()

    swaps = [
        (k_ref.at[:, columns(other, HEAD_DIM)], kraw.at[core]),
        (v_ref.at[:, columns(other, HEAD_DIM)], vbuf.at[chip + core]),
        (q_ref.at[:, columns(other, half)], q4.at[own_rows]),
        (do_ref.at[:, columns(other, half)], do4.at[own_rows]),
    ]
    swaps = [
        remote(src, dst, swap_send.at[i], swap_recv.at[i], peer)
        for i, (src, dst) in enumerate(swaps)
    ]

    tile_base = lax.div(seq, 2) * tile_total
    first, count = [], []
    for t in range(tile_total):
        begin = jnp.int32(images)
        total = jnp.int32(0)
        for i in range(images):
            flag = mask_ref[i, tile_base + t]
            total = total + flag
            begin = jnp.where((flag == 1) & (begin == images), i, begin)
        first.append(begin)
        count.append(total)

    def pick(values, t):
        out = values[0]
        for k in range(1, len(values)):
            out = jnp.where(t == k, values[k], out)
        return out

    def reads(t):
        begin = pick(first, t)
        total = pick(count, t)
        found = []
        for r in range(READ_MOST):
            image = jnp.minimum(begin + r, images - 1)
            length = jnp.where(r < total, tiles_ref[image] * TILE_TOK, 0)
            found.append((image, length))
        return found

    def gather_message(buf, which, number, parity, image, device):
        slot = (number - 1) * 2 + parity
        return remote(
            buf.at[image],
            buf.at[image],
            ag_send.at[which, slot],
            ag_recv.at[which, slot],
            device,
        )

    ahead = jnp.where(core == 0, right, left)
    behind = jnp.where(core == 0, left, right)

    def gather_ahead(buf, which, parity):
        return gather_message(buf, which, 6 + core, parity, chip + parity, ahead)

    def gather_behind(buf, which, parity):
        return gather_message(buf, which, 7 - core, parity, chip + parity, behind)

    def gather_across(buf, which, parity):
        return gather_message(buf, which, 4, parity, chip + parity, across)

    def gather_beside(buf, which, parity):
        device = jnp.where(parity == 0, left, right)
        return gather_message(buf, which, 1, parity, image_at(1 - z, x, parity), device)

    def gather_copy(buf, which, number, parity):
        if number == 6:
            image, device = image_at(z, x, parity), right
        elif number == 7:
            image, device = image_at(z, x, parity), left
        elif number == 4:
            image, device = image_at(z, x, parity), across
        elif number == 5:
            image, device = image_at(z, x - 1 + 2 * parity, parity), (right, left)[parity]
        elif number == 3:
            image, device = image_at(z, x - 1 + 2 * parity, parity), across
        elif number == 1:
            image, device = image_at(1 - z, x, parity), (left, right)[parity]
        else:
            image, device = image_at(1 - z, x + 1 - 2 * parity, parity), (left, right)[parity]
        return gather_message(buf, which, number, parity, image, device)

    def gather_own(buf, which):
        gather_ahead(buf, which, core).start()
        gather_across(buf, which, core).start()

    def gather_swapped(buf, which):
        gather_behind(buf, which, other).start()
        gather_across(buf, which, other).start()
        gather_ahead(buf, which, other).start()
        gather_behind(buf, which, core).start()

    def gather_second(buf, which):
        for parity in (core, other):
            gather_across(buf, which, parity).wait_recv()
            gather_beside(buf, which, parity).start()

    def gather_third(buf, which):
        for parity, source in ((0, 6), (1, 7)):
            gather_copy(buf, which, source, parity).wait_recv()
            gather_copy(buf, which, 5, parity).start()
            gather_copy(buf, which, 3, parity).start()

    def gather_fourth(buf, which):
        for parity in (0, 1):
            gather_copy(buf, which, 1, parity).wait_recv()
            gather_copy(buf, which, 2, parity).start()

    def gather_last(buf, which):
        for number, parity in (
            (6, 1), (7, 0), (5, 0), (5, 1), (3, 0), (3, 1), (2, 0), (2, 1),
        ):
            gather_copy(buf, which, number, parity).wait_recv()
        for number in range(1, 8):
            for parity in (0, 1):
                gather_copy(buf, which, number, parity).wait_send()

    key_gain = gains_ref[1:2, :]

    def norm_keys(parity):
        for s in range(subs):
            rows = slice(s * TILE_TOK, (s + 1) * TILE_TOK)
            entries = kraw[parity, rows, :].astype(F32)
            inverse = lax.rsqrt(jnp.mean(entries * entries, axis=-1, keepdims=True) + EPSILON)
            unit = entries * inverse
            unit_keys[parity, rows, :] = unit
            inverse_keys[parity, rows, :] = inverse
            kbuf[chip + parity, rows, :] = (unit * key_gain).astype(BF16)

    mine[0].wait()
    norm_keys(core)
    pl.semaphore_wait(barrier, len(greeted))
    swaps[0].start()
    gather_own(kbuf, 0)
    for copy in swaps[1:]:
        copy.start()
    swaps[0].wait_recv()
    norm_keys(other)
    gather_swapped(kbuf, 0)

    gcol[...] = jnp.transpose(jnp.broadcast_to(gains_ref[0:1, :], (HEAD_DIM, HEAD_DIM)))
    overlap[...] = jnp.zeros_like(overlap)
    for i in (2, 3):
        mine[i].wait()
        swaps[i].wait_recv()

    def prepare(t, carry):
        rows = columns(t, TEXT_TILE)
        gain_column = gcol[...]
        for h in range(group):
            cols = slice(h * HEAD_DIM, (h + 1) * HEAD_DIM)
            turned = jnp.transpose(q4[rows, cols].astype(F32))
            inverse = lax.rsqrt(jnp.mean(turned * turned, axis=0, keepdims=True) + EPSILON)
            unit = turned * inverse
            normed = unit * gain_column
            ut[t, :, cols] = unit
            rinv[t, :, cols] = inverse
            qnt[t, :, cols] = normed.astype(BF16)
            qn[t, cols, :] = jnp.transpose(normed).astype(BF16)
            cotangent = do4[rows, cols]
            don[t, cols, :] = cotangent
            dot_t[t, :, cols] = jnp.transpose(cotangent.astype(F32)).astype(BF16)

        return carry

    lax.fori_loop(0, tile_total, prepare, 0)
    gather_second(kbuf, 0)
    gather_third(kbuf, 0)
    gather_fourth(kbuf, 0)

    mine[1].wait()
    swaps[1].wait_recv()
    gather_own(vbuf, 1)
    gather_swapped(vbuf, 1)
    gather_last(kbuf, 0)

    def forward(t, carry):
        slots = reads(t)
        keys = [kbuf[image] for image, _ in slots]
        for pair in range(pairs):
            cols = slice(pair * pair_width, (pair + 1) * pair_width)
            turned = qnt[t, :, cols]
            scratch = sbuf.at[pair % 2]
            peak = jnp.full((1, pair_width), -1e30, F32)
            for r, (_, length) in enumerate(slots):
                scores = dot(keys[r], turned)
                scratch[r * max_tokens : (r + 1) * max_tokens, :] = scores
                for s in range(subs):
                    top = jnp.max(scores[s * TILE_TOK : (s + 1) * TILE_TOK], axis=0, keepdims=True)
                    peak = jnp.maximum(peak, jnp.where(s * TILE_TOK < length, top, -1e30))
            total = jnp.zeros((1, pair_width), F32)
            for r, (_, length) in enumerate(slots):
                for s in range(subs):
                    begin = r * max_tokens + s * TILE_TOK
                    shift = jnp.where(s * TILE_TOK < length, peak, 1e30)
                    powers = jnp.exp2(
                        (scratch[begin : begin + TILE_TOK, :] - shift) * (scale * LOG2E)
                    )
                    scratch[begin : begin + TILE_TOK, :] = powers
                    total = total + jnp.sum(powers, axis=0, keepdims=True)
            inverse = 1.0 / total
            for r in range(READ_MOST * subs):
                begin = r * TILE_TOK
                wbuf[t, begin : begin + TILE_TOK, cols] = (
                    scratch[begin : begin + TILE_TOK, :] * inverse
                ).astype(BF16)
        cotangents = don[t]
        for r in range(READ_MOST):
            rows = slice(r * max_tokens, (r + 1) * max_tokens)
            vslot[t, r] = dot(wbuf[t, rows, :], cotangents)

        @pl.when(t == 0)
        def _():
            gather_second(vbuf, 1)
            gather_third(vbuf, 1)

        @pl.when(t == 2)
        def _():
            gather_fourth(vbuf, 1)

        return carry

    lax.fori_loop(0, tile_total, forward, 0)

    def sum_route(number, parity):
        if number == 1:
            return image_at(1 - z, x + 1 - 2 * parity, parity), (right, left)[parity]
        if number == 2:
            return image_at(1 - z, x + 2, parity), (right, left)[parity]
        if number == 3:
            return image_at(1 - z, x - 1 + 2 * parity, parity), across
        if number == 4:
            return image_at(1 - z, x, parity), across
        if number == 5:
            return image_at(z, x + 2, parity), (left, right)[parity]
        if number == 6:
            return image_at(z, x - 1, parity), left
        return image_at(z, x + 1, parity), right

    def sum_copy(send, land, which, number, parity):
        image, device = sum_route(number, parity)
        slot = (number - 1) * 2 + parity
        return remote(
            send.at[image], land.at[slot], rs_send.at[which, slot], rs_recv.at[which, slot], device
        )

    def share(slot_ref, image, s):
        rows = slice(s * TILE_TOK, (s + 1) * TILE_TOK)
        value = None
        for t in range(tile_total):
            place = image - first[t]
            weight = jnp.where((place >= 0) & (place < count[t]), 1.0, 0.0).astype(F32)
            part = slot_ref[t, jnp.clip(place, 0, READ_MOST - 1), rows, :] * weight
            value = part if value is None else value + part
        return value

    def summed(slot_ref, land, image, sources, s):
        value = share(slot_ref, image, s)
        for number, parity in sources:
            slot = (number - 1) * 2 + parity
            value = value + land[slot, s * TILE_TOK : (s + 1) * TILE_TOK, :].astype(F32)
        return value

    def send_sum(slot_ref, send, land, which, number, parity, sources):
        for source_number, source_parity in sources:
            sum_copy(send, land, which, source_number, source_parity).wait_recv()
        image, _ = sum_route(number, parity)
        for s in range(subs):
            rows = slice(s * TILE_TOK, (s + 1) * TILE_TOK)
            send[image, rows, :] = summed(slot_ref, land, image, sources, s).astype(BF16)
        sum_copy(send, land, which, number, parity).start()

    def sum_far(*refs):
        send_sum(*refs, 2, 0, ())
        send_sum(*refs, 2, 1, ())

    def sum_level(*refs):
        send_sum(*refs, 3, 0, ())
        send_sum(*refs, 3, 1, ())

    def sum_middle(*refs):
        send_sum(*refs, 5, 0, ())
        send_sum(*refs, 5, 1, ())

    def sum_beside(*refs):
        send_sum(*refs, 1, 0, ((2, 0),))
        send_sum(*refs, 1, 1, ((2, 1),))

    def sum_near(*refs):
        send_sum(*refs, 7, 0, ())
        send_sum(*refs, 6, 1, ())

    def sum_across(*refs):
        send_sum(*refs, 4, 0, ((1, 0),))
        send_sum(*refs, 4, 1, ((1, 1),))

    def sum_end(*refs):
        send_sum(*refs, 6, 0, ((5, 0), (3, 0)))
        send_sum(*refs, 7, 1, ((5, 1), (3, 1)))

    root_sources = (4, 6, 7)

    root_messages = [(number, parity) for number in root_sources for parity in (0, 1)]

    def sum_last(send, land, which, arriving):
        for number, parity in arriving:
            sum_copy(send, land, which, number, parity).wait_recv()
        for number in range(1, 8):
            for parity in (0, 1):
                sum_copy(send, land, which, number, parity).wait_send()

    value_refs = (vslot, vsend, vland, 0)
    key_refs = (kslot, ksend, kland, 1)
    sum_far(*value_refs)
    sum_level(*value_refs)
    sum_middle(*value_refs)
    gather_last(vbuf, 1)

    def backward(t, carry):
        slots = reads(t)
        values = [vbuf[image] for image, _ in slots]
        values_turned = [jnp.transpose(value) for value in values]
        for pair in range(pairs):
            cols = slice(pair * pair_width, (pair + 1) * pair_width)
            cotangent = dot_t[t, :, cols]
            attended = None
            for r in range(READ_MOST):
                part = dot(
                    values_turned[r], wbuf[t, r * max_tokens : (r + 1) * max_tokens, cols]
                )
                attended = part if attended is None else attended + part
            oturn[t, :, cols] = attended.astype(BF16)
            row_dot = jnp.sum(attended * cotangent.astype(F32), axis=0, keepdims=True)
            for r in range(READ_MOST):
                rows = slice(r * max_tokens, (r + 1) * max_tokens)
                value_scores = dot(values[r], cotangent)
                wbuf[t, rows, cols] = (
                    wbuf[t, rows, cols].astype(F32) * (value_scores - row_dot)
                ).astype(BF16)
        normed = qn[t]
        for r, (image, _) in enumerate(slots):
            rows = slice(r * max_tokens, (r + 1) * max_tokens)
            part = dot(wbuf[t, rows, :], normed)
            kslot[t, r] = part
            product = part * kbuf[image].astype(F32)
            overlap[...] += jnp.sum(product.reshape(max_tokens // 8, 8, HEAD_DIM), axis=0)

        @pl.when(t == 0)
        def _():
            sum_beside(*value_refs)
            sum_near(*value_refs)

        return carry

    lax.fori_loop(0, tile_total, backward, 0)

    def gain_copy(buf, send, recv, place, k, device):
        return remote(buf.at[place], buf.at[place], send.at[k - 1], recv.at[place], device)

    def gain_start(buf, send, recv, place, total, device_of, value):
        buf[place] = value
        for k in range(1, total):
            gain_copy(buf, send, recv, place, k, device_of(k)).start()

    def gain_finish(buf, send, recv, place, total, device_of):
        for k in range(1, total):
            source = lax.rem(place + k, total)
            gain_copy(buf, send, recv, source, k, device_of(k)).wait_recv()
        for k in range(1, total):
            gain_copy(buf, send, recv, place, k, device_of(k)).wait_send()
        value = buf[0]
        for k in range(1, total):
            value = value + buf[k]
        return value

    z_stage = (zgain, zsend, zrecv, 2 * mp + z, chain, z_device)
    y_stage = (ygain, ysend, yrecv, dp, dp_total, y_device)
    core_stage = (cgain, csend, crecv, core, 2, lambda k: {"seq": peer})
    x_stage = (xgain, xsend, xrecv, x, RING, x_device)

    gain_start(*z_stage, overlap[...])
    sum_far(*key_refs)
    sum_end(*value_refs)
    sum_across(*value_refs)
    sum_level(*key_refs)

    def queries_backward(t, carry):
        slots = reads(t)
        gain_column = gcol[...]
        gain_pair = jnp.concatenate([gain_column, gain_column], axis=1)
        keys_turned = [jnp.transpose(kbuf[image]) for image, _ in slots]
        rows_out = columns(t, TEXT_TILE)
        for pair in range(pairs):
            cols = slice(pair * pair_width, (pair + 1) * pair_width)
            grads = None
            for r in range(READ_MOST):
                part = dot(keys_turned[r], wbuf[t, r * max_tokens : (r + 1) * max_tokens, cols])
                grads = part if grads is None else grads + part
            grads = grads * scale
            unit = ut[t, :, cols]
            scaled = grads * gain_pair
            mean = jnp.mean(scaled * unit, axis=0, keepdims=True)
            grad_query = rinv[t, :, cols] * (scaled - unit * mean)
            for h in range(2):
                head = slice(h * HEAD_DIM, (h + 1) * HEAD_DIM)
                out_cols = slice((2 * pair + h) * HEAD_DIM, (2 * pair + h + 1) * HEAD_DIM)
                obuf[rows_out, out_cols] = jnp.transpose(oturn[t, :, out_cols])
                dqbuf[rows_out, out_cols] = jnp.transpose(grad_query[:, head]).astype(BF16)

        @pl.when(t == 1)
        def _():
            sum_beside(*key_refs)
            sum_middle(*key_refs)
            sum_near(*key_refs)
            gain_start(*y_stage, gain_finish(*z_stage))

        @pl.when(t == 3)
        def _():
            gain_start(*core_stage, gain_finish(*y_stage))

        return carry

    lax.fori_loop(0, tile_total, queries_backward, 0)

    out_cols = columns(core, half)
    head_cols = columns(core, HEAD_DIM)
    results = [
        (obuf.at[own_rows], obuf.at[other_rows], o_out, out_cols),
        (dqbuf.at[own_rows], dqbuf.at[other_rows], dq_out, out_cols),
        (gvbuf.at[core], gvbuf.at[other], dv_out, head_cols),
        (gkbuf.at[core], gkbuf.at[other], dk_out, head_cols),
    ]
    locals_out = [
        pltpu.make_async_copy(own, out.at[:, cols], out_local.at[i])
        for i, (own, _, out, cols) in enumerate(results)
    ]
    remotes_out = [
        remote(theirs, out.at[:, cols], out_send.at[i], out_recv.at[i], peer)
        for i, (_, theirs, out, cols) in enumerate(results)
    ]

    def put_out(i):
        locals_out[i].start()
        remotes_out[i].start()

    put_out(0)
    put_out(1)

    def root_sum(slot_ref, land, parity, s):
        sources = [(number, parity) for number in root_sources]
        return summed(slot_ref, land, chip + parity, sources, s)

    sum_last(vsend, vland, 0, root_messages)
    for parity in (other, core):
        for s in range(subs):
            rows = slice(s * TILE_TOK, (s + 1) * TILE_TOK)
            gvbuf[parity, rows, :] = root_sum(vslot, vland, parity, s).astype(BF16)
    put_out(2)

    sum_across(*key_refs)
    gain_start(*x_stage, gain_finish(*core_stage))
    sum_end(*key_refs)
    for number, parity in ((7, 0), (6, 1)):
        sum_copy(ksend, kland, 1, number, parity).wait_recv()
        for s in range(subs):
            rows = slice(s * TILE_TOK, (s + 1) * TILE_TOK)
            early[parity, rows, :] = summed(kslot, kland, chip + parity, [(number, parity)], s)
    sum_last(ksend, kland, 1, ((4, 0), (4, 1), (6, 0), (7, 1)))
    for parity in (other, core):
        for s in range(subs):
            rows = slice(s * TILE_TOK, (s + 1) * TILE_TOK)
            grads = early[parity, rows, :]
            for slot in (6 + parity, 10 + 3 * parity):
                grads = grads + kland[slot, rows, :].astype(F32)
            grads = grads * scale
            unit = unit_keys[parity, rows, :]
            scaled = grads * key_gain
            mean = jnp.mean(scaled * unit, axis=-1, keepdims=True)
            gkbuf[parity, rows, :] = (
                inverse_keys[parity, rows, :] * (scaled - unit * mean)
            ).astype(BF16)
        if parity is other:
            remotes_out[3].start()
    locals_out[3].start()
    products = jnp.sum(gain_finish(*x_stage), axis=0, keepdims=True) * scale
    gain_out[...] = products / gains_ref[...]

    for copy in swaps:
        copy.wait_send()
    for i in range(len(results)):
        locals_out[i].wait()
        remotes_out[i].wait_send()
        remotes_out[i].wait_recv()


def mover(count, *refs):
    sources, targets = refs[:count], refs[count : 2 * count]
    stages, load_sem, store_sem = refs[2 * count : 3 * count], refs[-2], refs[-1]
    loads, stores = [], []
    for source, stage, target in zip(sources, stages, targets):
        cuts = MOVE_CUTS if source.shape[0] % (16 * MOVE_CUTS) == 0 else 1
        rows = source.shape[0] // cuts
        for k in range(cuts):
            cut = pl.ds(k * rows, rows)
            place = len(loads)
            loads.append(pltpu.make_async_copy(source.at[cut], stage.at[cut], load_sem.at[place]))
            stores.append(pltpu.make_async_copy(stage.at[cut], target.at[cut], store_sem.at[place]))
    for load in loads:
        load.start()
    for load, store in zip(loads, stores):
        load.wait()
        store.start()
    for store in stores:
        store.wait()


def on_device(
    dp_total,
    mp_total,
    queries,
    image_keys,
    image_values,
    norm_gains,
    image_tiles,
    read_mask,
    grad_attended,
):
    tokens, width = queries.shape[1:]
    max_tokens, kv_width = image_keys.shape[2:]
    group = width // kv_width
    images = read_mask.shape[2]
    half = group * HEAD_DIM
    tile_total = 2 * tokens // TEXT_TILE
    slot_width = READ_MOST * max_tokens
    hbm = pl.BlockSpec(memory_space=pl.ANY)
    vmem = pl.BlockSpec(memory_space=pltpu.VMEM)
    smem = pl.BlockSpec(memory_space=pltpu.SMEM)
    dma = pltpu.SemaphoreType.DMA
    block = (images, max_tokens, HEAD_DIM)
    slots = (tile_total, READ_MOST, max_tokens, HEAD_DIM)
    turned = (tile_total, HEAD_DIM, half)
    plain = (tile_total, half, HEAD_DIM)
    scratch = [
        pltpu.VMEM((2 * tokens, half), BF16),
        pltpu.VMEM((2 * tokens, half), BF16),
        pltpu.VMEM((2, max_tokens, HEAD_DIM), BF16),
        pltpu.VMEM(block, BF16),
        pltpu.VMEM(block, BF16),
        pltpu.VMEM(plain, BF16),
        pltpu.VMEM(turned, BF16),
        pltpu.VMEM(turned, BF16),
        pltpu.VMEM(plain, BF16),
        pltpu.VMEM(turned, F32),
        pltpu.VMEM((tile_total, 1, half), F32),
        pltpu.VMEM((tile_total, slot_width, half), BF16),
        pltpu.VMEM((2, slot_width, 2 * HEAD_DIM), F32),
        pltpu.VMEM(slots, F32),
        pltpu.VMEM(slots, F32),
        pltpu.VMEM(block, BF16),
        pltpu.VMEM(block, BF16),
        pltpu.VMEM((14, max_tokens, HEAD_DIM), BF16),
        pltpu.VMEM((14, max_tokens, HEAD_DIM), BF16),
        pltpu.VMEM((2 * tokens, half), BF16),
        pltpu.VMEM((2 * tokens, half), BF16),
        pltpu.VMEM((2, max_tokens, HEAD_DIM), BF16),
        pltpu.VMEM((2, max_tokens, HEAD_DIM), BF16),
        pltpu.VMEM((2, max_tokens, HEAD_DIM), F32),
        pltpu.VMEM((2, max_tokens, HEAD_DIM), F32),
        pltpu.VMEM((2, max_tokens, 1), F32),
        pltpu.VMEM(turned, BF16),
        pltpu.VMEM((8, HEAD_DIM), F32),
        pltpu.VMEM((HEAD_DIM, HEAD_DIM), F32),
        pltpu.VMEM((2 * mp_total, 8, HEAD_DIM), F32),
        pltpu.VMEM((dp_total, 8, HEAD_DIM), F32),
        pltpu.VMEM((2, 8, HEAD_DIM), F32),
        pltpu.VMEM((RING, 8, HEAD_DIM), F32),
        dma((4,)),
        dma((4,)),
        dma((4,)),
        dma((2, 14)),
        dma((2, 14)),
        dma((2, 14)),
        dma((2, 14)),
        dma((4,)),
        dma((4,)),
        dma((4,)),
        dma((2 * mp_total,)),
        dma((2 * mp_total,)),
        dma((dp_total,)),
        dma((dp_total,)),
        dma((2,)),
        dma((2,)),
        dma((RING,)),
        dma((RING,)),
    ]
    attended, grad_queries, grad_keys, grad_values, grad_gains = pl.pallas_call(
        functools.partial(kernel, images, group, dp_total, mp_total),
        out_shape=[
            jax.ShapeDtypeStruct((tokens, width), BF16),
            jax.ShapeDtypeStruct((tokens, width), BF16),
            jax.ShapeDtypeStruct((max_tokens, kv_width), BF16),
            jax.ShapeDtypeStruct((max_tokens, kv_width), BF16),
            jax.ShapeDtypeStruct((2, HEAD_DIM), F32),
        ],
        in_specs=[hbm, hbm, hbm, hbm, vmem, smem, smem],
        out_specs=[hbm, hbm, hbm, hbm, vmem],
        scratch_shapes=scratch,
        compiler_params=pltpu.CompilerParams(
            collective_id=0, has_side_effects=True, vmem_limit_bytes=60 * 1024 * 1024
        ),
    )(
        queries[0],
        grad_attended[0],
        image_keys[0, 0],
        image_values[0, 0],
        norm_gains,
        image_tiles[0],
        jnp.transpose(read_mask[0]),
    )
    results = (attended, grad_queries, grad_keys, grad_values, grad_gains)
    attended, grad_queries, grad_keys, grad_values, grad_gains = pl.pallas_call(
        functools.partial(mover, len(results)),
        out_shape=[jax.ShapeDtypeStruct(part.shape, part.dtype) for part in results],
        in_specs=[hbm] * len(results),
        out_specs=[hbm] * len(results),
        scratch_shapes=[pltpu.VMEM(part.shape, part.dtype) for part in results]
        + [dma((MOVE_CUTS * len(results),))] * 2,
        compiler_params=pltpu.CompilerParams(vmem_limit_bytes=60 * 1024 * 1024),
    )(*results)
    return (
        attended[None],
        grad_queries[None],
        grad_keys[None, None],
        grad_values[None, None],
        grad_gains,
    )


def solution(mesh):
    in_specs = (
        P("dp", "seq", "mp"),
        P("dp", "seq", None, "mp"),
        P("dp", "seq", None, "mp"),
        P(),
        P("dp", None),
        P("dp", None, None),
        P("dp", "seq", "mp"),
    )
    out_specs = (
        P("dp", "seq", "mp"),
        P("dp", "seq", "mp"),
        P("dp", "seq", None, "mp"),
        P("dp", "seq", None, "mp"),
        P(),
    )
    per_device = functools.partial(on_device, mesh.shape["dp"], mesh.shape["mp"])
    return jax.shard_map(
        per_device, mesh=mesh, in_specs=in_specs, out_specs=out_specs, check_vma=False
    )
```

```python
import functools

import jax
import jax.numpy as jnp
from jax import lax
from jax.experimental import pallas as pl
from jax.experimental.pallas import tpu as pltpu
from jax.sharding import PartitionSpec as P

HEAD_DIM = 128
TEXT_TILE = 128
TILE_TOK = 128
READ_MOST = 3
EPSILON = 1e-05
LOG2E = 1.4426950408889634
MESH = pl.DeviceIdType.MESH
BF16 = jnp.bfloat16
MOVE_CUTS = 4
F32 = jnp.float32

RING = 4


def dot(a, b):
    return jnp.dot(a, b, preferred_element_type=F32)


def kernel(
    images,
    group,
    dp_total,
    mp_total,
    q_ref,
    do_ref,
    k_ref,
    v_ref,
    gains_ref,
    tiles_ref,
    mask_ref,
    o_out,
    dq_out,
    dk_out,
    dv_out,
    gain_out,
    q4,
    do4,
    kraw,
    kbuf,
    vbuf,
    qn,
    qnt,
    dot_t,
    don,
    ut,
    rinv,
    wbuf,
    sbuf,
    vslot,
    kslot,
    vsend,
    ksend,
    vland,
    kland,
    obuf,
    dqbuf,
    gkbuf,
    gvbuf,
    early,
    unit_keys,
    inverse_keys,
    oturn,
    overlap,
    gcol,
    member_gain,
    cross_gain,
    total_gain,
    local_sem,
    swap_send,
    swap_recv,
    ag_send,
    ag_recv,
    rs_send,
    rs_recv,
    out_local,
    out_send,
    out_recv,
    ready_sem,
    member_send,
    member_recv,
    cross_send,
    cross_recv,
    total_send,
    total_recv,
):
    max_tokens = k_ref.shape[0]
    tokens = q_ref.shape[0]
    half = group * HEAD_DIM
    pair_width = 2 * HEAD_DIM
    pairs = group // 2
    tile_total = 2 * tokens // TEXT_TILE
    subs = max_tokens // TILE_TOK
    scale = HEAD_DIM ** (-0.5)

    seq = lax.axis_index("seq")
    core = lax.rem(seq, 2)
    x = lax.rem(lax.div(seq, 2), RING)
    z = lax.div(seq, 2 * RING)
    other = 1 - core

    def image_at(zz, xx, parity):
        return zz * (2 * RING) + lax.rem(xx + RING, RING) * 2 + parity

    peer = image_at(z, x, other)
    dp = lax.axis_index("dp")
    mp = lax.axis_index("mp")
    right = image_at(z, x + 1, core)
    left = image_at(z, x - 1, core)
    across = image_at(1 - z, x, core)
    chip = image_at(z, x, 0)

    def columns(index, width):
        return pl.ds(pl.multiple_of(index * width, width), width)

    own_rows = columns(core, tokens)
    other_rows = columns(other, tokens)

    def remote(src, dst, send_sem, recv_sem, device):
        device = device if isinstance(device, dict) else {"seq": device}
        return pltpu.make_async_remote_copy(
            src_ref=src,
            dst_ref=dst,
            send_sem=send_sem,
            recv_sem=recv_sem,
            device_id=device,
            device_id_type=MESH,
        )

    barrier = pltpu.get_barrier_semaphore()
    leader = seq == 0
    members = 2 * 2 * RING
    group_total = dp_total * mp_total
    group_place = dp * mp_total + mp

    def cross_device(k):
        place = lax.rem(group_place + k, group_total)
        return {"dp": lax.div(place, mp_total), "mp": lax.rem(place, mp_total)}

    neighbours = (peer, right, left, across)
    for device in neighbours:

        @pl.when(device != 0)
        def _():
            pl.semaphore_signal(barrier, inc=1, device_id={"seq": device}, device_id_type=MESH)

    @pl.when(leader)
    def _():
        for k in range(1, group_total):
            pl.semaphore_signal(barrier, inc=1, device_id=cross_device(k), device_id_type=MESH)

    def enter():
        @pl.when(leader)
        def _():
            pl.semaphore_wait(ready_sem, len(neighbours))

        @pl.when(jnp.logical_not(leader))
        def _():
            pl.semaphore_wait(barrier, len(neighbours))

        for device in neighbours:

            @pl.when(device == 0)
            def _():
                pl.semaphore_signal(
                    ready_sem, inc=1, device_id={"seq": device}, device_id_type=MESH
                )

    mine = [
        pltpu.make_async_copy(k_ref.at[:, columns(core, HEAD_DIM)], kraw.at[core], local_sem.at[0]),
        pltpu.make_async_copy(
            v_ref.at[:, columns(core, HEAD_DIM)], vbuf.at[chip + core], local_sem.at[1]
        ),
        pltpu.make_async_copy(q_ref.at[:, columns(core, half)], q4.at[own_rows], local_sem.at[2]),
        pltpu.make_async_copy(do_ref.at[:, columns(core, half)], do4.at[own_rows], local_sem.at[3]),
    ]
    for copy in mine:
        copy.start()

    swaps = [
        (k_ref.at[:, columns(other, HEAD_DIM)], kraw.at[core]),
        (v_ref.at[:, columns(other, HEAD_DIM)], vbuf.at[chip + core]),
        (q_ref.at[:, columns(other, half)], q4.at[own_rows]),
        (do_ref.at[:, columns(other, half)], do4.at[own_rows]),
    ]
    swaps = [
        remote(src, dst, swap_send.at[i], swap_recv.at[i], peer)
        for i, (src, dst) in enumerate(swaps)
    ]

    tile_base = lax.div(seq, 2) * tile_total
    first, count = [], []
    for t in range(tile_total):
        begin = jnp.int32(images)
        total = jnp.int32(0)
        for i in range(images):
            flag = mask_ref[i, tile_base + t]
            total = total + flag
            begin = jnp.where((flag == 1) & (begin == images), i, begin)
        first.append(begin)
        count.append(total)

    def pick(values, t):
        out = values[0]
        for k in range(1, len(values)):
            out = jnp.where(t == k, values[k], out)
        return out

    def reads(t):
        begin = pick(first, t)
        total = pick(count, t)
        found = []
        for r in range(READ_MOST):
            image = jnp.minimum(begin + r, images - 1)
            length = jnp.where(r < total, tiles_ref[image] * TILE_TOK, 0)
            found.append((image, length))
        return found

    def gather_message(buf, which, number, parity, image, device):
        slot = (number - 1) * 2 + parity
        return remote(
            buf.at[image],
            buf.at[image],
            ag_send.at[which, slot],
            ag_recv.at[which, slot],
            device,
        )

    ahead = jnp.where(core == 0, right, left)
    behind = jnp.where(core == 0, left, right)

    def gather_ahead(buf, which, parity):
        return gather_message(buf, which, 6 + core, parity, chip + parity, ahead)

    def gather_behind(buf, which, parity):
        return gather_message(buf, which, 7 - core, parity, chip + parity, behind)

    def gather_across(buf, which, parity):
        return gather_message(buf, which, 4, parity, chip + parity, across)

    def gather_beside(buf, which, parity):
        device = jnp.where(parity == 0, left, right)
        return gather_message(buf, which, 1, parity, image_at(1 - z, x, parity), device)

    def gather_copy(buf, which, number, parity):
        if number == 6:
            image, device = image_at(z, x, parity), right
        elif number == 7:
            image, device = image_at(z, x, parity), left
        elif number == 4:
            image, device = image_at(z, x, parity), across
        elif number == 5:
            image, device = image_at(z, x - 1 + 2 * parity, parity), (right, left)[parity]
        elif number == 3:
            image, device = image_at(z, x - 1 + 2 * parity, parity), across
        elif number == 1:
            image, device = image_at(1 - z, x, parity), (left, right)[parity]
        else:
            image, device = image_at(1 - z, x + 1 - 2 * parity, parity), (left, right)[parity]
        return gather_message(buf, which, number, parity, image, device)

    def gather_own(buf, which):
        gather_ahead(buf, which, core).start()
        gather_across(buf, which, core).start()

    def gather_swapped(buf, which):
        gather_behind(buf, which, other).start()
        gather_across(buf, which, other).start()
        gather_ahead(buf, which, other).start()
        gather_behind(buf, which, core).start()

    def gather_second(buf, which):
        for parity in (core, other):
            gather_across(buf, which, parity).wait_recv()
            gather_beside(buf, which, parity).start()

    def gather_third(buf, which):
        for parity, source in ((0, 6), (1, 7)):
            gather_copy(buf, which, source, parity).wait_recv()
            gather_copy(buf, which, 5, parity).start()
            gather_copy(buf, which, 3, parity).start()

    def gather_fourth(buf, which):
        for parity in (0, 1):
            gather_copy(buf, which, 1, parity).wait_recv()
            gather_copy(buf, which, 2, parity).start()

    def gather_last(buf, which):
        for number, parity in (
            (6, 1), (7, 0), (5, 0), (5, 1), (3, 0), (3, 1), (2, 0), (2, 1),
        ):
            gather_copy(buf, which, number, parity).wait_recv()
        for number in range(1, 8):
            for parity in (0, 1):
                gather_copy(buf, which, number, parity).wait_send()

    key_gain = gains_ref[1:2, :]

    def norm_keys(parity):
        for s in range(subs):
            rows = slice(s * TILE_TOK, (s + 1) * TILE_TOK)
            entries = kraw[parity, rows, :].astype(F32)
            inverse = lax.rsqrt(jnp.mean(entries * entries, axis=-1, keepdims=True) + EPSILON)
            unit = entries * inverse
            unit_keys[parity, rows, :] = unit
            inverse_keys[parity, rows, :] = inverse
            kbuf[chip + parity, rows, :] = (unit * key_gain).astype(BF16)

    mine[0].wait()
    norm_keys(core)
    enter()
    swaps[0].start()
    gather_own(kbuf, 0)
    for copy in swaps[1:]:
        copy.start()
    swaps[0].wait_recv()
    norm_keys(other)
    gather_swapped(kbuf, 0)

    gcol[...] = jnp.transpose(jnp.broadcast_to(gains_ref[0:1, :], (HEAD_DIM, HEAD_DIM)))
    overlap[...] = jnp.zeros_like(overlap)
    for i in (2, 3):
        mine[i].wait()
        swaps[i].wait_recv()

    def prepare(t, carry):
        rows = columns(t, TEXT_TILE)
        gain_column = gcol[...]
        for h in range(group):
            cols = slice(h * HEAD_DIM, (h + 1) * HEAD_DIM)
            turned = jnp.transpose(q4[rows, cols].astype(F32))
            inverse = lax.rsqrt(jnp.mean(turned * turned, axis=0, keepdims=True) + EPSILON)
            unit = turned * inverse
            normed = unit * gain_column
            ut[t, :, cols] = unit
            rinv[t, :, cols] = inverse
            qnt[t, :, cols] = normed.astype(BF16)
            qn[t, cols, :] = jnp.transpose(normed).astype(BF16)
            cotangent = do4[rows, cols]
            don[t, cols, :] = cotangent
            dot_t[t, :, cols] = jnp.transpose(cotangent.astype(F32)).astype(BF16)

        return carry

    lax.fori_loop(0, tile_total, prepare, 0)
    gather_second(kbuf, 0)
    gather_third(kbuf, 0)
    gather_fourth(kbuf, 0)

    mine[1].wait()
    swaps[1].wait_recv()
    gather_own(vbuf, 1)
    gather_swapped(vbuf, 1)
    gather_last(kbuf, 0)

    def forward(t, carry):
        slots = reads(t)
        keys = [kbuf[image] for image, _ in slots]
        for pair in range(pairs):
            cols = slice(pair * pair_width, (pair + 1) * pair_width)
            turned = qnt[t, :, cols]
            scratch = sbuf.at[pair % 2]
            peak = jnp.full((1, pair_width), -1e30, F32)
            for r, (_, length) in enumerate(slots):
                scores = dot(keys[r], turned)
                scratch[r * max_tokens : (r + 1) * max_tokens, :] = scores
                for s in range(subs):
                    top = jnp.max(scores[s * TILE_TOK : (s + 1) * TILE_TOK], axis=0, keepdims=True)
                    peak = jnp.maximum(peak, jnp.where(s * TILE_TOK < length, top, -1e30))
            total = jnp.zeros((1, pair_width), F32)
            for r, (_, length) in enumerate(slots):
                for s in range(subs):
                    begin = r * max_tokens + s * TILE_TOK
                    shift = jnp.where(s * TILE_TOK < length, peak, 1e30)
                    powers = jnp.exp2(
                        (scratch[begin : begin + TILE_TOK, :] - shift) * (scale * LOG2E)
                    )
                    scratch[begin : begin + TILE_TOK, :] = powers
                    total = total + jnp.sum(powers, axis=0, keepdims=True)
            inverse = 1.0 / total
            for r in range(READ_MOST * subs):
                begin = r * TILE_TOK
                wbuf[t, begin : begin + TILE_TOK, cols] = (
                    scratch[begin : begin + TILE_TOK, :] * inverse
                ).astype(BF16)
        cotangents = don[t]
        for r in range(READ_MOST):
            rows = slice(r * max_tokens, (r + 1) * max_tokens)
            vslot[t, r] = dot(wbuf[t, rows, :], cotangents)

        @pl.when(t == 0)
        def _():
            gather_second(vbuf, 1)
            gather_third(vbuf, 1)

        @pl.when(t == 2)
        def _():
            gather_fourth(vbuf, 1)

        return carry

    lax.fori_loop(0, tile_total, forward, 0)

    def sum_route(number, parity):
        if number == 1:
            return image_at(1 - z, x + 1 - 2 * parity, parity), (right, left)[parity]
        if number == 2:
            return image_at(1 - z, x + 2, parity), (right, left)[parity]
        if number == 3:
            return image_at(1 - z, x - 1 + 2 * parity, parity), across
        if number == 4:
            return image_at(1 - z, x, parity), across
        if number == 5:
            return image_at(z, x + 2, parity), (left, right)[parity]
        if number == 6:
            return image_at(z, x - 1, parity), left
        return image_at(z, x + 1, parity), right

    def sum_copy(send, land, which, number, parity):
        image, device = sum_route(number, parity)
        slot = (number - 1) * 2 + parity
        return remote(
            send.at[image], land.at[slot], rs_send.at[which, slot], rs_recv.at[which, slot], device
        )

    def share(slot_ref, image, s):
        rows = slice(s * TILE_TOK, (s + 1) * TILE_TOK)
        value = None
        for t in range(tile_total):
            place = image - first[t]
            weight = jnp.where((place >= 0) & (place < count[t]), 1.0, 0.0).astype(F32)
            part = slot_ref[t, jnp.clip(place, 0, READ_MOST - 1), rows, :] * weight
            value = part if value is None else value + part
        return value

    def summed(slot_ref, land, image, sources, s):
        value = share(slot_ref, image, s)
        for number, parity in sources:
            slot = (number - 1) * 2 + parity
            value = value + land[slot, s * TILE_TOK : (s + 1) * TILE_TOK, :].astype(F32)
        return value

    def send_sum(slot_ref, send, land, which, number, parity, sources):
        for source_number, source_parity in sources:
            sum_copy(send, land, which, source_number, source_parity).wait_recv()
        image, _ = sum_route(number, parity)
        for s in range(subs):
            rows = slice(s * TILE_TOK, (s + 1) * TILE_TOK)
            send[image, rows, :] = summed(slot_ref, land, image, sources, s).astype(BF16)
        sum_copy(send, land, which, number, parity).start()

    def sum_far(*refs):
        send_sum(*refs, 2, 0, ())
        send_sum(*refs, 2, 1, ())

    def sum_level(*refs):
        send_sum(*refs, 3, 0, ())
        send_sum(*refs, 3, 1, ())

    def sum_middle(*refs):
        send_sum(*refs, 5, 0, ())
        send_sum(*refs, 5, 1, ())

    def sum_beside(*refs):
        send_sum(*refs, 1, 0, ((2, 0),))
        send_sum(*refs, 1, 1, ((2, 1),))

    def sum_near(*refs):
        send_sum(*refs, 7, 0, ())
        send_sum(*refs, 6, 1, ())

    def sum_across(*refs):
        send_sum(*refs, 4, 0, ((1, 0),))
        send_sum(*refs, 4, 1, ((1, 1),))

    def sum_end(*refs):
        send_sum(*refs, 6, 0, ((5, 0), (3, 0)))
        send_sum(*refs, 7, 1, ((5, 1), (3, 1)))

    root_sources = (4, 6, 7)

    root_messages = [(number, parity) for number in root_sources for parity in (0, 1)]

    def sum_last(send, land, which, arriving):
        for number, parity in arriving:
            sum_copy(send, land, which, number, parity).wait_recv()
        for number in range(1, 8):
            for parity in (0, 1):
                sum_copy(send, land, which, number, parity).wait_send()

    value_refs = (vslot, vsend, vland, 0)
    key_refs = (kslot, ksend, kland, 1)
    sum_far(*value_refs)
    sum_level(*value_refs)
    sum_middle(*value_refs)
    gather_last(vbuf, 1)

    def backward(t, carry):
        slots = reads(t)
        values = [vbuf[image] for image, _ in slots]
        values_turned = [jnp.transpose(value) for value in values]
        for pair in range(pairs):
            cols = slice(pair * pair_width, (pair + 1) * pair_width)
            cotangent = dot_t[t, :, cols]
            attended = None
            for r in range(READ_MOST):
                part = dot(
                    values_turned[r], wbuf[t, r * max_tokens : (r + 1) * max_tokens, cols]
                )
                attended = part if attended is None else attended + part
            oturn[t, :, cols] = attended.astype(BF16)
            row_dot = jnp.sum(attended * cotangent.astype(F32), axis=0, keepdims=True)
            for r in range(READ_MOST):
                rows = slice(r * max_tokens, (r + 1) * max_tokens)
                value_scores = dot(values[r], cotangent)
                wbuf[t, rows, cols] = (
                    wbuf[t, rows, cols].astype(F32) * (value_scores - row_dot)
                ).astype(BF16)
        normed = qn[t]
        for r, (image, _) in enumerate(slots):
            rows = slice(r * max_tokens, (r + 1) * max_tokens)
            part = dot(wbuf[t, rows, :], normed)
            kslot[t, r] = part
            product = part * kbuf[image].astype(F32)
            overlap[...] += jnp.sum(product.reshape(max_tokens // 8, 8, HEAD_DIM), axis=0)

        @pl.when(t == 0)
        def _():
            sum_beside(*value_refs)
            sum_near(*value_refs)

        return carry

    lax.fori_loop(0, tile_total, backward, 0)

    def member_copy(member):
        return remote(
            overlap, member_gain.at[member], member_send, member_recv.at[member], 0
        )

    def cross_copy(place, k):
        return remote(
            cross_gain.at[place],
            cross_gain.at[place],
            cross_send.at[k],
            cross_recv.at[place],
            cross_device(k),
        )

    def total_copy(member):
        return remote(total_gain, total_gain, total_send.at[member], total_recv, member)

    def in_order(buf, total):
        value = buf[0]
        for k in range(1, total):
            value = value + buf[k]
        return value

    def lead_gather():
        member_gain[0] = overlap[...]
        for member in range(1, members):
            member_copy(member).wait_recv()
        cross_gain[group_place] = in_order(member_gain, members)
        if group_total > 1:
            pl.semaphore_wait(barrier, group_total - 1)
        for k in range(1, group_total):
            cross_copy(group_place, k).start()

    def lead_spread():
        for k in range(1, group_total):
            cross_copy(lax.rem(group_place + k, group_total), k).wait_recv()
        total_gain[...] = in_order(cross_gain, group_total)
        for member in range(1, members):
            total_copy(member).start()

    @pl.when(jnp.logical_not(leader))
    def _():
        member_copy(seq).start()

    sum_far(*key_refs)
    sum_end(*value_refs)

    pl.when(leader)(lead_gather)

    sum_across(*value_refs)
    sum_level(*key_refs)

    def queries_backward(t, carry):
        slots = reads(t)
        gain_column = gcol[...]
        gain_pair = jnp.concatenate([gain_column, gain_column], axis=1)
        keys_turned = [jnp.transpose(kbuf[image]) for image, _ in slots]
        rows_out = columns(t, TEXT_TILE)
        for pair in range(pairs):
            cols = slice(pair * pair_width, (pair + 1) * pair_width)
            grads = None
            for r in range(READ_MOST):
                part = dot(keys_turned[r], wbuf[t, r * max_tokens : (r + 1) * max_tokens, cols])
                grads = part if grads is None else grads + part
            grads = grads * scale
            unit = ut[t, :, cols]
            scaled = grads * gain_pair
            mean = jnp.mean(scaled * unit, axis=0, keepdims=True)
            grad_query = rinv[t, :, cols] * (scaled - unit * mean)
            for h in range(2):
                head = slice(h * HEAD_DIM, (h + 1) * HEAD_DIM)
                out_cols = slice((2 * pair + h) * HEAD_DIM, (2 * pair + h + 1) * HEAD_DIM)
                obuf[rows_out, out_cols] = jnp.transpose(oturn[t, :, out_cols])
                dqbuf[rows_out, out_cols] = jnp.transpose(grad_query[:, head]).astype(BF16)

        @pl.when(t == 1)
        def _():
            sum_beside(*key_refs)
            sum_middle(*key_refs)
            sum_near(*key_refs)

        return carry

    lax.fori_loop(0, tile_total, queries_backward, 0)

    out_cols = columns(core, half)
    head_cols = columns(core, HEAD_DIM)
    results = [
        (obuf.at[own_rows], obuf.at[other_rows], o_out, out_cols),
        (dqbuf.at[own_rows], dqbuf.at[other_rows], dq_out, out_cols),
        (gvbuf.at[core], gvbuf.at[other], dv_out, head_cols),
        (gkbuf.at[core], gkbuf.at[other], dk_out, head_cols),
    ]
    locals_out = [
        pltpu.make_async_copy(own, out.at[:, cols], out_local.at[i])
        for i, (own, _, out, cols) in enumerate(results)
    ]
    remotes_out = [
        remote(theirs, out.at[:, cols], out_send.at[i], out_recv.at[i], peer)
        for i, (_, theirs, out, cols) in enumerate(results)
    ]

    def put_out(i):
        locals_out[i].start()
        remotes_out[i].start()

    put_out(0)
    put_out(1)

    def root_sum(slot_ref, land, parity, s):
        sources = [(number, parity) for number in root_sources]
        return summed(slot_ref, land, chip + parity, sources, s)

    sum_last(vsend, vland, 0, root_messages)
    for parity in (other, core):
        for s in range(subs):
            rows = slice(s * TILE_TOK, (s + 1) * TILE_TOK)
            gvbuf[parity, rows, :] = root_sum(vslot, vland, parity, s).astype(BF16)
    put_out(2)

    pl.when(leader)(lead_spread)

    sum_across(*key_refs)
    sum_end(*key_refs)
    for number, parity in ((7, 0), (6, 1)):
        sum_copy(ksend, kland, 1, number, parity).wait_recv()
        for s in range(subs):
            rows = slice(s * TILE_TOK, (s + 1) * TILE_TOK)
            early[parity, rows, :] = summed(kslot, kland, chip + parity, [(number, parity)], s)
    sum_last(ksend, kland, 1, ((4, 0), (4, 1), (6, 0), (7, 1)))
    for parity in (other, core):
        for s in range(subs):
            rows = slice(s * TILE_TOK, (s + 1) * TILE_TOK)
            grads = early[parity, rows, :]
            for slot in (6 + parity, 10 + 3 * parity):
                grads = grads + kland[slot, rows, :].astype(F32)
            grads = grads * scale
            unit = unit_keys[parity, rows, :]
            scaled = grads * key_gain
            mean = jnp.mean(scaled * unit, axis=-1, keepdims=True)
            gkbuf[parity, rows, :] = (
                inverse_keys[parity, rows, :] * (scaled - unit * mean)
            ).astype(BF16)
        if parity is other:
            remotes_out[3].start()
    locals_out[3].start()
    @pl.when(jnp.logical_not(leader))
    def _():
        total_copy(0).wait_recv()
        member_copy(seq).wait_send()

    @pl.when(leader)
    def _():
        for k in range(1, group_total):
            cross_copy(group_place, k).wait_send()
        for member in range(1, members):
            total_copy(member).wait_send()

    products = jnp.sum(total_gain[...], axis=0, keepdims=True) * scale
    gain_out[...] = products / gains_ref[...]

    for copy in swaps:
        copy.wait_send()
    for i in range(len(results)):
        locals_out[i].wait()
        remotes_out[i].wait_send()
        remotes_out[i].wait_recv()


def mover(count, *refs):
    sources, targets = refs[:count], refs[count : 2 * count]
    stages, load_sem, store_sem = refs[2 * count : 3 * count], refs[-2], refs[-1]
    loads, stores = [], []
    for source, stage, target in zip(sources, stages, targets):
        cuts = MOVE_CUTS if source.shape[0] % (16 * MOVE_CUTS) == 0 else 1
        rows = source.shape[0] // cuts
        for k in range(cuts):
            cut = pl.ds(k * rows, rows)
            place = len(loads)
            loads.append(pltpu.make_async_copy(source.at[cut], stage.at[cut], load_sem.at[place]))
            stores.append(pltpu.make_async_copy(stage.at[cut], target.at[cut], store_sem.at[place]))
    for load in loads:
        load.start()
    for load, store in zip(loads, stores):
        load.wait()
        store.start()
    for store in stores:
        store.wait()


def on_device(
    dp_total,
    mp_total,
    queries,
    image_keys,
    image_values,
    norm_gains,
    image_tiles,
    read_mask,
    grad_attended,
):
    tokens, width = queries.shape[1:]
    max_tokens, kv_width = image_keys.shape[2:]
    group = width // kv_width
    images = read_mask.shape[2]
    half = group * HEAD_DIM
    tile_total = 2 * tokens // TEXT_TILE
    slot_width = READ_MOST * max_tokens
    hbm = pl.BlockSpec(memory_space=pl.ANY)
    vmem = pl.BlockSpec(memory_space=pltpu.VMEM)
    smem = pl.BlockSpec(memory_space=pltpu.SMEM)
    dma = pltpu.SemaphoreType.DMA
    block = (images, max_tokens, HEAD_DIM)
    slots = (tile_total, READ_MOST, max_tokens, HEAD_DIM)
    turned = (tile_total, HEAD_DIM, half)
    plain = (tile_total, half, HEAD_DIM)
    scratch = [
        pltpu.VMEM((2 * tokens, half), BF16),
        pltpu.VMEM((2 * tokens, half), BF16),
        pltpu.VMEM((2, max_tokens, HEAD_DIM), BF16),
        pltpu.VMEM(block, BF16),
        pltpu.VMEM(block, BF16),
        pltpu.VMEM(plain, BF16),
        pltpu.VMEM(turned, BF16),
        pltpu.VMEM(turned, BF16),
        pltpu.VMEM(plain, BF16),
        pltpu.VMEM(turned, F32),
        pltpu.VMEM((tile_total, 1, half), F32),
        pltpu.VMEM((tile_total, slot_width, half), BF16),
        pltpu.VMEM((2, slot_width, 2 * HEAD_DIM), F32),
        pltpu.VMEM(slots, F32),
        pltpu.VMEM(slots, F32),
        pltpu.VMEM(block, BF16),
        pltpu.VMEM(block, BF16),
        pltpu.VMEM((14, max_tokens, HEAD_DIM), BF16),
        pltpu.VMEM((14, max_tokens, HEAD_DIM), BF16),
        pltpu.VMEM((2 * tokens, half), BF16),
        pltpu.VMEM((2 * tokens, half), BF16),
        pltpu.VMEM((2, max_tokens, HEAD_DIM), BF16),
        pltpu.VMEM((2, max_tokens, HEAD_DIM), BF16),
        pltpu.VMEM((2, max_tokens, HEAD_DIM), F32),
        pltpu.VMEM((2, max_tokens, HEAD_DIM), F32),
        pltpu.VMEM((2, max_tokens, 1), F32),
        pltpu.VMEM(turned, BF16),
        pltpu.VMEM((8, HEAD_DIM), F32),
        pltpu.VMEM((HEAD_DIM, HEAD_DIM), F32),
        pltpu.VMEM((4 * RING, 8, HEAD_DIM), F32),
        pltpu.VMEM((dp_total * mp_total, 8, HEAD_DIM), F32),
        pltpu.VMEM((8, HEAD_DIM), F32),
        dma((4,)),
        dma((4,)),
        dma((4,)),
        dma((2, 14)),
        dma((2, 14)),
        dma((2, 14)),
        dma((2, 14)),
        dma((4,)),
        dma((4,)),
        dma((4,)),
        pltpu.SemaphoreType.REGULAR,
        dma(()),
        dma((4 * RING,)),
        dma((dp_total * mp_total,)),
        dma((dp_total * mp_total,)),
        dma((4 * RING,)),
        dma(()),
    ]
    attended, grad_queries, grad_keys, grad_values, grad_gains = pl.pallas_call(
        functools.partial(kernel, images, group, dp_total, mp_total),
        out_shape=[
            jax.ShapeDtypeStruct((tokens, width), BF16),
            jax.ShapeDtypeStruct((tokens, width), BF16),
            jax.ShapeDtypeStruct((max_tokens, kv_width), BF16),
            jax.ShapeDtypeStruct((max_tokens, kv_width), BF16),
            jax.ShapeDtypeStruct((2, HEAD_DIM), F32),
        ],
        in_specs=[hbm, hbm, hbm, hbm, vmem, smem, smem],
        out_specs=[hbm, hbm, hbm, hbm, vmem],
        scratch_shapes=scratch,
        compiler_params=pltpu.CompilerParams(
            collective_id=0, has_side_effects=True, vmem_limit_bytes=60 * 1024 * 1024
        ),
    )(
        queries[0],
        grad_attended[0],
        image_keys[0, 0],
        image_values[0, 0],
        norm_gains,
        image_tiles[0],
        jnp.transpose(read_mask[0]),
    )
    results = (attended, grad_queries, grad_keys, grad_values, grad_gains)
    attended, grad_queries, grad_keys, grad_values, grad_gains = pl.pallas_call(
        functools.partial(mover, len(results)),
        out_shape=[jax.ShapeDtypeStruct(part.shape, part.dtype) for part in results],
        in_specs=[hbm] * len(results),
        out_specs=[hbm] * len(results),
        scratch_shapes=[pltpu.VMEM(part.shape, part.dtype) for part in results]
        + [dma((MOVE_CUTS * len(results),))] * 2,
        compiler_params=pltpu.CompilerParams(vmem_limit_bytes=60 * 1024 * 1024),
    )(*results)
    return (
        attended[None],
        grad_queries[None],
        grad_keys[None, None],
        grad_values[None, None],
        grad_gains,
    )


def solution(mesh):
    in_specs = (
        P("dp", "seq", "mp"),
        P("dp", "seq", None, "mp"),
        P("dp", "seq", None, "mp"),
        P(),
        P("dp", None),
        P("dp", None, None),
        P("dp", "seq", "mp"),
    )
    out_specs = (
        P("dp", "seq", "mp"),
        P("dp", "seq", "mp"),
        P("dp", "seq", None, "mp"),
        P("dp", "seq", None, "mp"),
        P(),
    )
    per_device = functools.partial(on_device, mesh.shape["dp"], mesh.shape["mp"])
    return jax.shard_map(
        per_device, mesh=mesh, in_specs=in_specs, out_specs=out_specs, check_vma=False
    )
```

```python
import functools

import jax
import jax.numpy as jnp
from jax import lax
from jax.experimental import pallas as pl
from jax.experimental.pallas import tpu as pltpu
from jax.sharding import PartitionSpec as P

HEAD_DIM = 128
TEXT_TILE = 128
TILE_TOK = 128
READ_MOST = 3
EPSILON = 1e-05
LOG2E = 1.4426950408889634
MESH = pl.DeviceIdType.MESH
BF16 = jnp.bfloat16
MOVE_CUTS = 4
F32 = jnp.float32

RING = 4


def dot(a, b):
    return jnp.dot(a, b, preferred_element_type=F32)


def kernel(
    images,
    group,
    dp_total,
    mp_total,
    q_ref,
    do_ref,
    k_ref,
    v_ref,
    gains_ref,
    tiles_ref,
    mask_ref,
    o_out,
    dq_out,
    dk_out,
    dv_out,
    gain_out,
    q4,
    do4,
    kraw,
    kbuf,
    vbuf,
    qn,
    qnt,
    dot_t,
    don,
    ut,
    rinv,
    wbuf,
    sbuf,
    vslot,
    kslot,
    vsend,
    ksend,
    vland,
    kland,
    obuf,
    dqbuf,
    gkbuf,
    gvbuf,
    early,
    mirror,
    peer_share,
    kother,
    unit_keys,
    inverse_keys,
    oturn,
    overlap,
    gcol,
    member_gain,
    cross_gain,
    total_gain,
    local_sem,
    swap_send,
    swap_recv,
    ag_send,
    ag_recv,
    rs_send,
    rs_recv,
    out_local,
    out_send,
    out_recv,
    share_sems,
    ready_sem,
    member_send,
    member_recv,
    cross_send,
    cross_recv,
    total_send,
    total_recv,
):
    max_tokens = k_ref.shape[0]
    tokens = q_ref.shape[0]
    half = group * HEAD_DIM
    pair_width = 2 * HEAD_DIM
    pairs = group // 2
    tile_total = 2 * tokens // TEXT_TILE
    subs = max_tokens // TILE_TOK
    scale = HEAD_DIM ** (-0.5)

    seq = lax.axis_index("seq")
    core = lax.rem(seq, 2)
    x = lax.rem(lax.div(seq, 2), RING)
    z = lax.div(seq, 2 * RING)
    other = 1 - core

    def image_at(zz, xx, parity):
        return zz * (2 * RING) + lax.rem(xx + RING, RING) * 2 + parity

    peer = image_at(z, x, other)
    dp = lax.axis_index("dp")
    mp = lax.axis_index("mp")
    right = image_at(z, x + 1, core)
    left = image_at(z, x - 1, core)
    across = image_at(1 - z, x, core)
    chip = image_at(z, x, 0)

    def columns(index, width):
        return pl.ds(pl.multiple_of(index * width, width), width)

    own_rows = columns(core, tokens)
    other_rows = columns(other, tokens)

    def remote(src, dst, send_sem, recv_sem, device):
        device = device if isinstance(device, dict) else {"seq": device}
        return pltpu.make_async_remote_copy(
            src_ref=src,
            dst_ref=dst,
            send_sem=send_sem,
            recv_sem=recv_sem,
            device_id=device,
            device_id_type=MESH,
        )

    barrier = pltpu.get_barrier_semaphore()
    leader = seq == 0
    members = 2 * 2 * RING
    group_total = dp_total * mp_total
    group_place = dp * mp_total + mp

    def cross_device(k):
        place = lax.rem(group_place + k, group_total)
        return {"dp": lax.div(place, mp_total), "mp": lax.rem(place, mp_total)}

    neighbours = (peer, right, left, across)
    for device in neighbours:

        @pl.when(device != 0)
        def _():
            pl.semaphore_signal(barrier, inc=1, device_id={"seq": device}, device_id_type=MESH)

    @pl.when(leader)
    def _():
        for k in range(1, group_total):
            pl.semaphore_signal(barrier, inc=1, device_id=cross_device(k), device_id_type=MESH)

    def enter():
        @pl.when(leader)
        def _():
            pl.semaphore_wait(ready_sem, len(neighbours))

        @pl.when(jnp.logical_not(leader))
        def _():
            pl.semaphore_wait(barrier, len(neighbours))

        for device in neighbours:

            @pl.when(device == 0)
            def _():
                pl.semaphore_signal(
                    ready_sem, inc=1, device_id={"seq": device}, device_id_type=MESH
                )

    mine = [
        pltpu.make_async_copy(k_ref.at[:, columns(core, HEAD_DIM)], kraw.at[core], local_sem.at[0]),
        pltpu.make_async_copy(
            v_ref.at[:, columns(core, HEAD_DIM)], vbuf.at[chip + core], local_sem.at[1]
        ),
        pltpu.make_async_copy(q_ref.at[:, columns(core, half)], q4.at[own_rows], local_sem.at[2]),
        pltpu.make_async_copy(do_ref.at[:, columns(core, half)], do4.at[own_rows], local_sem.at[3]),
        pltpu.make_async_copy(k_ref.at[:, columns(other, HEAD_DIM)], kother, local_sem.at[4]),
    ]
    for copy in mine:
        copy.start()

    swaps = [
        (k_ref.at[:, columns(other, HEAD_DIM)], kraw.at[core]),
        (v_ref.at[:, columns(other, HEAD_DIM)], vbuf.at[chip + core]),
        (q_ref.at[:, columns(other, half)], q4.at[own_rows]),
        (do_ref.at[:, columns(other, half)], do4.at[own_rows]),
    ]
    swaps = [
        remote(src, dst, swap_send.at[i], swap_recv.at[i], peer)
        for i, (src, dst) in enumerate(swaps)
    ]

    tile_base = lax.div(seq, 2) * tile_total
    first, count = [], []
    for t in range(tile_total):
        begin = jnp.int32(images)
        total = jnp.int32(0)
        for i in range(images):
            flag = mask_ref[i, tile_base + t]
            total = total + flag
            begin = jnp.where((flag == 1) & (begin == images), i, begin)
        first.append(begin)
        count.append(total)

    def pick(values, t):
        out = values[0]
        for k in range(1, len(values)):
            out = jnp.where(t == k, values[k], out)
        return out

    def reads(t):
        begin = pick(first, t)
        total = pick(count, t)
        found = []
        for r in range(READ_MOST):
            image = jnp.minimum(begin + r, images - 1)
            length = jnp.where(r < total, tiles_ref[image] * TILE_TOK, 0)
            found.append((image, length))
        return found

    def gather_message(buf, which, number, parity, image, device):
        slot = (number - 1) * 2 + parity
        return remote(
            buf.at[image],
            buf.at[image],
            ag_send.at[which, slot],
            ag_recv.at[which, slot],
            device,
        )

    ahead = jnp.where(core == 0, right, left)
    behind = jnp.where(core == 0, left, right)

    def gather_ahead(buf, which, parity):
        return gather_message(buf, which, 6 + core, parity, chip + parity, ahead)

    def gather_behind(buf, which, parity):
        return gather_message(buf, which, 7 - core, parity, chip + parity, behind)

    def gather_across(buf, which, parity):
        return gather_message(buf, which, 4, parity, chip + parity, across)

    def gather_beside(buf, which, parity):
        device = jnp.where(parity == 0, left, right)
        return gather_message(buf, which, 1, parity, image_at(1 - z, x, parity), device)

    def gather_copy(buf, which, number, parity):
        if number == 6:
            image, device = image_at(z, x, parity), right
        elif number == 7:
            image, device = image_at(z, x, parity), left
        elif number == 4:
            image, device = image_at(z, x, parity), across
        elif number == 5:
            image, device = image_at(z, x - 1 + 2 * parity, parity), (right, left)[parity]
        elif number == 3:
            image, device = image_at(z, x - 1 + 2 * parity, parity), across
        elif number == 1:
            image, device = image_at(1 - z, x, parity), (left, right)[parity]
        else:
            image, device = image_at(1 - z, x + 1 - 2 * parity, parity), (left, right)[parity]
        return gather_message(buf, which, number, parity, image, device)

    def gather_own(buf, which):
        gather_ahead(buf, which, core).start()
        gather_across(buf, which, core).start()

    def gather_swapped(buf, which):
        gather_behind(buf, which, other).start()
        gather_across(buf, which, other).start()
        gather_ahead(buf, which, other).start()
        gather_behind(buf, which, core).start()

    def gather_second(buf, which):
        for parity in (core, other):
            gather_across(buf, which, parity).wait_recv()
            gather_beside(buf, which, parity).start()

    def gather_third(buf, which):
        for parity, source in ((0, 6), (1, 7)):
            gather_copy(buf, which, source, parity).wait_recv()
            gather_copy(buf, which, 5, parity).start()
            gather_copy(buf, which, 3, parity).start()

    def gather_fourth(buf, which):
        for parity in (0, 1):
            gather_copy(buf, which, 1, parity).wait_recv()
            gather_copy(buf, which, 2, parity).start()

    def gather_last(buf, which):
        for number, parity in (
            (6, 1), (7, 0), (5, 0), (5, 1), (3, 0), (3, 1), (2, 0), (2, 1),
        ):
            gather_copy(buf, which, number, parity).wait_recv()
        for number in range(1, 8):
            for parity in (0, 1):
                gather_copy(buf, which, number, parity).wait_send()

    key_gain = gains_ref[1:2, :]

    def norm_rows(entries, place, rows):
        inverse = lax.rsqrt(jnp.mean(entries * entries, axis=-1, keepdims=True) + EPSILON)
        unit = entries * inverse
        if place is not None:
            unit_keys[place, rows, :] = unit
            inverse_keys[place, rows, :] = inverse
        return unit

    def norm_keys(parity, place):
        for s in range(subs):
            rows = slice(s * TILE_TOK, (s + 1) * TILE_TOK)
            unit = norm_rows(kraw[parity, rows, :].astype(F32), place, rows)
            kbuf[chip + parity, rows, :] = (unit * key_gain).astype(BF16)

    mine[0].wait()
    norm_keys(core, core)
    enter()
    swaps[0].start()
    gather_own(kbuf, 0)
    for copy in swaps[1:]:
        copy.start()
    swaps[0].wait_recv()
    norm_keys(other, None)
    gather_swapped(kbuf, 0)

    gcol[...] = jnp.transpose(jnp.broadcast_to(gains_ref[0:1, :], (HEAD_DIM, HEAD_DIM)))
    overlap[...] = jnp.zeros_like(overlap)
    for i in (2, 3):
        mine[i].wait()
        swaps[i].wait_recv()

    def prepare(t, carry):
        rows = columns(t, TEXT_TILE)
        gain_column = gcol[...]
        for h in range(group):
            cols = slice(h * HEAD_DIM, (h + 1) * HEAD_DIM)
            turned = jnp.transpose(q4[rows, cols].astype(F32))
            inverse = lax.rsqrt(jnp.mean(turned * turned, axis=0, keepdims=True) + EPSILON)
            unit = turned * inverse
            normed = unit * gain_column
            ut[t, :, cols] = unit
            rinv[t, :, cols] = inverse
            qnt[t, :, cols] = normed.astype(BF16)
            qn[t, cols, :] = jnp.transpose(normed).astype(BF16)
            cotangent = do4[rows, cols]
            don[t, cols, :] = cotangent
            dot_t[t, :, cols] = jnp.transpose(cotangent.astype(F32)).astype(BF16)

        return carry

    lax.fori_loop(0, tile_total, prepare, 0)

    mine[4].wait()
    for s in range(subs):
        rows = slice(s * TILE_TOK, (s + 1) * TILE_TOK)
        norm_rows(kother[rows, :].astype(F32), other, rows)

    gather_second(kbuf, 0)
    gather_third(kbuf, 0)
    mine[1].wait()
    swaps[1].wait_recv()
    gather_across(vbuf, 1, core).start()
    gather_across(vbuf, 1, other).start()
    gather_fourth(kbuf, 0)
    gather_ahead(vbuf, 1, core).start()
    gather_behind(vbuf, 1, other).start()
    gather_ahead(vbuf, 1, other).start()
    gather_behind(vbuf, 1, core).start()
    gather_last(kbuf, 0)

    def forward(t, carry):
        slots = reads(t)
        keys = [kbuf[image] for image, _ in slots]
        for pair in range(pairs):
            cols = slice(pair * pair_width, (pair + 1) * pair_width)
            turned = qnt[t, :, cols]
            scratch = sbuf.at[pair % 2]
            peak = jnp.full((1, pair_width), -1e30, F32)
            for r, (_, length) in enumerate(slots):
                scores = dot(keys[r], turned)
                scratch[r * max_tokens : (r + 1) * max_tokens, :] = scores
                for s in range(subs):
                    top = jnp.max(scores[s * TILE_TOK : (s + 1) * TILE_TOK], axis=0, keepdims=True)
                    peak = jnp.maximum(peak, jnp.where(s * TILE_TOK < length, top, -1e30))
            total = jnp.zeros((1, pair_width), F32)
            for r, (_, length) in enumerate(slots):
                for s in range(subs):
                    begin = r * max_tokens + s * TILE_TOK
                    shift = jnp.where(s * TILE_TOK < length, peak, 1e30)
                    powers = jnp.exp2(
                        (scratch[begin : begin + TILE_TOK, :] - shift) * (scale * LOG2E)
                    )
                    scratch[begin : begin + TILE_TOK, :] = powers
                    total = total + jnp.sum(powers, axis=0, keepdims=True)
            inverse = 1.0 / total
            for r in range(READ_MOST * subs):
                begin = r * TILE_TOK
                wbuf[t, begin : begin + TILE_TOK, cols] = (
                    scratch[begin : begin + TILE_TOK, :] * inverse
                ).astype(BF16)
        cotangents = don[t]
        for r in range(READ_MOST):
            rows = slice(r * max_tokens, (r + 1) * max_tokens)
            vslot[t, r] = dot(wbuf[t, rows, :], cotangents)

        @pl.when(t == 0)
        def _():
            gather_second(vbuf, 1)
            gather_third(vbuf, 1)

        @pl.when(t == 2)
        def _():
            gather_fourth(vbuf, 1)

        return carry

    lax.fori_loop(0, tile_total, forward, 0)

    def sum_route(number, parity):
        if number == 1:
            return image_at(1 - z, x + 1 - 2 * parity, parity), (right, left)[parity]
        if number == 2:
            return image_at(1 - z, x + 2, parity), (right, left)[parity]
        if number == 3:
            return image_at(1 - z, x - 1 + 2 * parity, parity), across
        if number == 4:
            return image_at(1 - z, x, parity), across
        if number == 5:
            return image_at(z, x + 2, parity), (left, right)[parity]
        if number == 6:
            return image_at(z, x - 1, parity), left
        return image_at(z, x + 1, parity), right

    def sum_copy(send, land, which, number, parity):
        image, device = sum_route(number, parity)
        slot = (number - 1) * 2 + parity
        place = slot
        if which == 1 and number in (4, 6, 7):
            place = (number - 1) * 2 + core
            device = device - core + parity
        return remote(
            send.at[image], land.at[place], rs_send.at[which, slot], rs_recv.at[which, place], device
        )

    def root_wait(send, land, which, number, head):
        place = (number - 1) * 2 + head
        remote(
            send.at[0], land.at[place], rs_send.at[which, 0], rs_recv.at[which, place], across
        ).wait_recv()

    def share(slot_ref, image, s):
        rows = slice(s * TILE_TOK, (s + 1) * TILE_TOK)
        value = None
        for t in range(tile_total):
            place = image - first[t]
            weight = jnp.where((place >= 0) & (place < count[t]), 1.0, 0.0).astype(F32)
            part = slot_ref[t, jnp.clip(place, 0, READ_MOST - 1), rows, :] * weight
            value = part if value is None else value + part
        return value

    def summed(slot_ref, land, image, sources, s):
        value = share(slot_ref, image, s)
        for number, parity in sources:
            slot = (number - 1) * 2 + parity
            value = value + land[slot, s * TILE_TOK : (s + 1) * TILE_TOK, :].astype(F32)
        return value

    def send_sum(slot_ref, send, land, which, number, parity, sources):
        for source_number, source_parity in sources:
            sum_copy(send, land, which, source_number, source_parity).wait_recv()
        image, _ = sum_route(number, parity)
        for s in range(subs):
            rows = slice(s * TILE_TOK, (s + 1) * TILE_TOK)
            send[image, rows, :] = summed(slot_ref, land, image, sources, s).astype(BF16)
        sum_copy(send, land, which, number, parity).start()

    def sum_far(*refs):
        send_sum(*refs, 2, 0, ())
        send_sum(*refs, 2, 1, ())

    def sum_level(*refs):
        send_sum(*refs, 3, 0, ())
        send_sum(*refs, 3, 1, ())

    def sum_middle(*refs):
        send_sum(*refs, 5, 0, ())
        send_sum(*refs, 5, 1, ())

    def sum_beside(*refs):
        send_sum(*refs, 1, 0, ((2, 0),))
        send_sum(*refs, 1, 1, ((2, 1),))

    def sum_near(*refs):
        send_sum(*refs, 7, 0, ())
        send_sum(*refs, 6, 1, ())

    def sum_across(*refs):
        send_sum(*refs, 4, 0, ((1, 0),))
        send_sum(*refs, 4, 1, ((1, 1),))

    def sum_end(*refs):
        send_sum(*refs, 6, 0, ((5, 0), (3, 0)))
        send_sum(*refs, 7, 1, ((5, 1), (3, 1)))

    root_sources = (4, 6, 7)

    root_messages = [(number, parity) for number in root_sources for parity in (0, 1)]

    def sum_last(send, land, which, arriving):
        for number, parity in arriving:
            sum_copy(send, land, which, number, parity).wait_recv()
        for number in range(1, 8):
            for parity in (0, 1):
                sum_copy(send, land, which, number, parity).wait_send()

    value_refs = (vslot, vsend, vland, 0)
    key_refs = (kslot, ksend, kland, 1)
    sum_far(*value_refs)
    sum_level(*value_refs)
    sum_middle(*value_refs)
    gather_last(vbuf, 1)

    def backward(t, carry):
        slots = reads(t)
        values = [vbuf[image] for image, _ in slots]
        values_turned = [jnp.transpose(value) for value in values]
        for pair in range(pairs):
            cols = slice(pair * pair_width, (pair + 1) * pair_width)
            cotangent = dot_t[t, :, cols]
            attended = None
            for r in range(READ_MOST):
                part = dot(
                    values_turned[r], wbuf[t, r * max_tokens : (r + 1) * max_tokens, cols]
                )
                attended = part if attended is None else attended + part
            oturn[t, :, cols] = attended.astype(BF16)
            row_dot = jnp.sum(attended * cotangent.astype(F32), axis=0, keepdims=True)
            for r in range(READ_MOST):
                rows = slice(r * max_tokens, (r + 1) * max_tokens)
                value_scores = dot(values[r], cotangent)
                wbuf[t, rows, cols] = (
                    wbuf[t, rows, cols].astype(F32) * (value_scores - row_dot)
                ).astype(BF16)
        normed = qn[t]
        for r, (image, _) in enumerate(slots):
            rows = slice(r * max_tokens, (r + 1) * max_tokens)
            part = dot(wbuf[t, rows, :], normed)
            kslot[t, r] = part
            product = part * kbuf[image].astype(F32)
            overlap[...] += jnp.sum(product.reshape(max_tokens // 8, 8, HEAD_DIM), axis=0)

        @pl.when(t == 0)
        def _():
            sum_beside(*value_refs)
            sum_near(*value_refs)

        return carry

    lax.fori_loop(0, tile_total, backward, 0)

    def member_copy(member):
        return remote(
            overlap, member_gain.at[member], member_send, member_recv.at[member], 0
        )

    def cross_copy(place, k):
        return remote(
            cross_gain.at[place],
            cross_gain.at[place],
            cross_send.at[k],
            cross_recv.at[place],
            cross_device(k),
        )

    def total_copy(member):
        return remote(total_gain, total_gain, total_send.at[member], total_recv, member)

    def in_order(buf, total):
        value = buf[0]
        for k in range(1, total):
            value = value + buf[k]
        return value

    def lead_gather():
        member_gain[0] = overlap[...]
        for member in range(1, members):
            member_copy(member).wait_recv()
        cross_gain[group_place] = in_order(member_gain, members)
        if group_total > 1:
            pl.semaphore_wait(barrier, group_total - 1)
        for k in range(1, group_total):
            cross_copy(group_place, k).start()

    def lead_spread():
        for k in range(1, group_total):
            cross_copy(lax.rem(group_place + k, group_total), k).wait_recv()
        total_gain[...] = in_order(cross_gain, group_total)
        for member in range(1, members):
            total_copy(member).start()

    @pl.when(jnp.logical_not(leader))
    def _():
        member_copy(seq).start()

    sum_far(*key_refs)
    sum_end(*value_refs)

    pl.when(leader)(lead_gather)

    sum_across(*value_refs)
    sum_level(*key_refs)

    def queries_backward(t, carry):
        slots = reads(t)
        gain_column = gcol[...]
        gain_pair = jnp.concatenate([gain_column, gain_column], axis=1)
        keys_turned = [jnp.transpose(kbuf[image]) for image, _ in slots]
        rows_out = columns(t, TEXT_TILE)
        for pair in range(pairs):
            cols = slice(pair * pair_width, (pair + 1) * pair_width)
            grads = None
            for r in range(READ_MOST):
                part = dot(keys_turned[r], wbuf[t, r * max_tokens : (r + 1) * max_tokens, cols])
                grads = part if grads is None else grads + part
            grads = grads * scale
            unit = ut[t, :, cols]
            scaled = grads * gain_pair
            mean = jnp.mean(scaled * unit, axis=0, keepdims=True)
            grad_query = rinv[t, :, cols] * (scaled - unit * mean)
            for h in range(2):
                head = slice(h * HEAD_DIM, (h + 1) * HEAD_DIM)
                out_cols = slice((2 * pair + h) * HEAD_DIM, (2 * pair + h + 1) * HEAD_DIM)
                obuf[rows_out, out_cols] = jnp.transpose(oturn[t, :, out_cols])
                dqbuf[rows_out, out_cols] = jnp.transpose(grad_query[:, head]).astype(BF16)

        @pl.when(t == 1)
        def _():
            sum_beside(*key_refs)
            sum_middle(*key_refs)
            sum_near(*key_refs)

        return carry

    lax.fori_loop(0, tile_total, queries_backward, 0)

    out_cols = columns(core, half)
    head_cols = columns(core, HEAD_DIM)
    results = [
        (obuf.at[own_rows], obuf.at[other_rows], o_out, out_cols),
        (dqbuf.at[own_rows], dqbuf.at[other_rows], dq_out, out_cols),
        (gvbuf.at[core], gvbuf.at[other], dv_out, head_cols),
    ]
    locals_out = [
        pltpu.make_async_copy(own, out.at[:, cols], out_local.at[i])
        for i, (own, _, out, cols) in enumerate(results)
    ]
    remotes_out = [
        remote(theirs, out.at[:, cols], out_send.at[i], out_recv.at[i], peer)
        for i, (_, theirs, out, cols) in enumerate(results)
    ]

    def put_out(i):
        locals_out[i].start()
        remotes_out[i].start()

    put_out(0)
    put_out(1)

    def root_sum(slot_ref, land, parity, s):
        sources = [(number, parity) for number in root_sources]
        return summed(slot_ref, land, chip + parity, sources, s)

    sum_last(vsend, vland, 0, root_messages)
    for parity in (other, core):
        for s in range(subs):
            rows = slice(s * TILE_TOK, (s + 1) * TILE_TOK)
            gvbuf[parity, rows, :] = root_sum(vslot, vland, parity, s).astype(BF16)
    put_out(2)

    pl.when(leader)(lead_spread)

    for s in range(subs):
        rows = slice(s * TILE_TOK, (s + 1) * TILE_TOK)
        mirror[rows, :] = share(kslot, chip + other, s)
        early[core, rows, :] = share(kslot, chip + core, s)
    share_copy = remote(mirror, peer_share, share_sems.at[0], share_sems.at[1], peer)
    share_copy.start()
    sum_across(*key_refs)
    sum_end(*key_refs)
    share_copy.wait()
    near, late = 7 - core, 6 + core
    for head in (0, 1):
        root_wait(ksend, kland, 1, near, head)
    for s in range(subs):
        rows = slice(s * TILE_TOK, (s + 1) * TILE_TOK)
        place = (near - 1) * 2
        early[core, rows, :] += kland[place + core, rows, :].astype(F32)
        early[other, rows, :] = peer_share[rows, :] + kland[place + other, rows, :].astype(F32)
    for number in (4, late):
        for head in (0, 1):
            root_wait(ksend, kland, 1, number, head)
    sum_last(ksend, kland, 1, ())
    last_out = []
    for head in (0, 1):
        for s in range(subs):
            rows = slice(s * TILE_TOK, (s + 1) * TILE_TOK)
            grads = early[head, rows, :]
            for number in (4, late):
                grads = grads + kland[(number - 1) * 2 + head, rows, :].astype(F32)
            grads = grads * scale
            unit = unit_keys[head, rows, :]
            scaled = grads * key_gain
            mean = jnp.mean(scaled * unit, axis=-1, keepdims=True)
            gkbuf[head, rows, :] = (
                inverse_keys[head, rows, :] * (scaled - unit * mean)
            ).astype(BF16)
        last_out.append(
            pltpu.make_async_copy(
                gkbuf.at[head],
                dk_out.at[:, head * HEAD_DIM : (head + 1) * HEAD_DIM],
                out_local.at[3 + head],
            )
        )
        last_out[head].start()
    @pl.when(jnp.logical_not(leader))
    def _():
        total_copy(0).wait_recv()
        member_copy(seq).wait_send()

    @pl.when(leader)
    def _():
        for k in range(1, group_total):
            cross_copy(group_place, k).wait_send()
        for member in range(1, members):
            total_copy(member).wait_send()

    products = jnp.sum(total_gain[...], axis=0, keepdims=True) * scale
    gain_out[...] = products / gains_ref[...]

    for copy in swaps:
        copy.wait_send()
    for copy in last_out:
        copy.wait()
    for i in range(len(results)):
        locals_out[i].wait()
        remotes_out[i].wait_send()
        remotes_out[i].wait_recv()


def mover(count, *refs):
    sources, targets = refs[:count], refs[count : 2 * count]
    stages, load_sem, store_sem = refs[2 * count : 3 * count], refs[-2], refs[-1]
    loads, stores = [], []
    for source, stage, target in zip(sources, stages, targets):
        cuts = MOVE_CUTS if source.shape[0] % (16 * MOVE_CUTS) == 0 else 1
        rows = source.shape[0] // cuts
        for k in range(cuts):
            cut = pl.ds(k * rows, rows)
            place = len(loads)
            loads.append(pltpu.make_async_copy(source.at[cut], stage.at[cut], load_sem.at[place]))
            stores.append(pltpu.make_async_copy(stage.at[cut], target.at[cut], store_sem.at[place]))
    for load in loads:
        load.start()
    for load, store in zip(loads, stores):
        load.wait()
        store.start()
    for store in stores:
        store.wait()


def on_device(
    dp_total,
    mp_total,
    queries,
    image_keys,
    image_values,
    norm_gains,
    image_tiles,
    read_mask,
    grad_attended,
):
    tokens, width = queries.shape[1:]
    max_tokens, kv_width = image_keys.shape[2:]
    group = width // kv_width
    images = read_mask.shape[2]
    half = group * HEAD_DIM
    tile_total = 2 * tokens // TEXT_TILE
    slot_width = READ_MOST * max_tokens
    hbm = pl.BlockSpec(memory_space=pl.ANY)
    vmem = pl.BlockSpec(memory_space=pltpu.VMEM)
    smem = pl.BlockSpec(memory_space=pltpu.SMEM)
    dma = pltpu.SemaphoreType.DMA
    block = (images, max_tokens, HEAD_DIM)
    slots = (tile_total, READ_MOST, max_tokens, HEAD_DIM)
    turned = (tile_total, HEAD_DIM, half)
    plain = (tile_total, half, HEAD_DIM)
    scratch = [
        pltpu.VMEM((2 * tokens, half), BF16),
        pltpu.VMEM((2 * tokens, half), BF16),
        pltpu.VMEM((2, max_tokens, HEAD_DIM), BF16),
        pltpu.VMEM(block, BF16),
        pltpu.VMEM(block, BF16),
        pltpu.VMEM(plain, BF16),
        pltpu.VMEM(turned, BF16),
        pltpu.VMEM(turned, BF16),
        pltpu.VMEM(plain, BF16),
        pltpu.VMEM(turned, F32),
        pltpu.VMEM((tile_total, 1, half), F32),
        pltpu.VMEM((tile_total, slot_width, half), BF16),
        pltpu.VMEM((2, slot_width, 2 * HEAD_DIM), F32),
        pltpu.VMEM(slots, F32),
        pltpu.VMEM(slots, F32),
        pltpu.VMEM(block, BF16),
        pltpu.VMEM(block, BF16),
        pltpu.VMEM((14, max_tokens, HEAD_DIM), BF16),
        pltpu.VMEM((14, max_tokens, HEAD_DIM), BF16),
        pltpu.VMEM((2 * tokens, half), BF16),
        pltpu.VMEM((2 * tokens, half), BF16),
        pltpu.VMEM((2, max_tokens, HEAD_DIM), BF16),
        pltpu.VMEM((2, max_tokens, HEAD_DIM), BF16),
        pltpu.VMEM((2, max_tokens, HEAD_DIM), F32),
        pltpu.VMEM((max_tokens, HEAD_DIM), F32),
        pltpu.VMEM((max_tokens, HEAD_DIM), F32),
        pltpu.VMEM((max_tokens, HEAD_DIM), BF16),
        pltpu.VMEM((2, max_tokens, HEAD_DIM), F32),
        pltpu.VMEM((2, max_tokens, 1), F32),
        pltpu.VMEM(turned, BF16),
        pltpu.VMEM((8, HEAD_DIM), F32),
        pltpu.VMEM((HEAD_DIM, HEAD_DIM), F32),
        pltpu.VMEM((4 * RING, 8, HEAD_DIM), F32),
        pltpu.VMEM((dp_total * mp_total, 8, HEAD_DIM), F32),
        pltpu.VMEM((8, HEAD_DIM), F32),
        dma((5,)),
        dma((5,)),
        dma((5,)),
        dma((2, 14)),
        dma((2, 14)),
        dma((2, 14)),
        dma((2, 14)),
        dma((5,)),
        dma((4,)),
        dma((4,)),
        dma((2,)),
        pltpu.SemaphoreType.REGULAR,
        dma(()),
        dma((4 * RING,)),
        dma((dp_total * mp_total,)),
        dma((dp_total * mp_total,)),
        dma((4 * RING,)),
        dma(()),
    ]
    attended, grad_queries, grad_keys, grad_values, grad_gains = pl.pallas_call(
        functools.partial(kernel, images, group, dp_total, mp_total),
        out_shape=[
            jax.ShapeDtypeStruct((tokens, width), BF16),
            jax.ShapeDtypeStruct((tokens, width), BF16),
            jax.ShapeDtypeStruct((max_tokens, kv_width), BF16),
            jax.ShapeDtypeStruct((max_tokens, kv_width), BF16),
            jax.ShapeDtypeStruct((2, HEAD_DIM), F32),
        ],
        in_specs=[hbm, hbm, hbm, hbm, vmem, smem, smem],
        out_specs=[hbm, hbm, hbm, hbm, vmem],
        scratch_shapes=scratch,
        compiler_params=pltpu.CompilerParams(
            collective_id=0, has_side_effects=True, vmem_limit_bytes=60 * 1024 * 1024
        ),
    )(
        queries[0],
        grad_attended[0],
        image_keys[0, 0],
        image_values[0, 0],
        norm_gains,
        image_tiles[0],
        jnp.transpose(read_mask[0]),
    )
    results = (attended, grad_queries, grad_keys, grad_values, grad_gains)
    attended, grad_queries, grad_keys, grad_values, grad_gains = pl.pallas_call(
        functools.partial(mover, len(results)),
        out_shape=[jax.ShapeDtypeStruct(part.shape, part.dtype) for part in results],
        in_specs=[hbm] * len(results),
        out_specs=[hbm] * len(results),
        scratch_shapes=[pltpu.VMEM(part.shape, part.dtype) for part in results]
        + [dma((MOVE_CUTS * len(results),))] * 2,
        compiler_params=pltpu.CompilerParams(vmem_limit_bytes=60 * 1024 * 1024),
    )(*results)
    return (
        attended[None],
        grad_queries[None],
        grad_keys[None, None],
        grad_values[None, None],
        grad_gains,
    )


def solution(mesh):
    in_specs = (
        P("dp", "seq", "mp"),
        P("dp", "seq", None, "mp"),
        P("dp", "seq", None, "mp"),
        P(),
        P("dp", None),
        P("dp", None, None),
        P("dp", "seq", "mp"),
    )
    out_specs = (
        P("dp", "seq", "mp"),
        P("dp", "seq", "mp"),
        P("dp", "seq", None, "mp"),
        P("dp", "seq", None, "mp"),
        P(),
    )
    per_device = functools.partial(on_device, mesh.shape["dp"], mesh.shape["mp"])
    return jax.shard_map(
        per_device, mesh=mesh, in_specs=in_specs, out_specs=out_specs, check_vma=False
    )
```

```python
import functools

import jax
import jax.numpy as jnp
from jax import lax
from jax.experimental import pallas as pl
from jax.experimental.pallas import tpu as pltpu
from jax.sharding import PartitionSpec as P

HEAD_DIM = 128
TEXT_TILE = 128
TILE_TOK = 128
READ_MOST = 3
EPSILON = 1e-05
LOG2E = 1.4426950408889634
MESH = pl.DeviceIdType.MESH
BF16 = jnp.bfloat16
MOVE_CUTS = 2
F32 = jnp.float32

RING = 4


def dot(a, b):
    return jnp.dot(a, b, preferred_element_type=F32)


def kernel(
    images,
    group,
    dp_total,
    mp_total,
    q_ref,
    do_ref,
    k_ref,
    v_ref,
    gains_ref,
    tiles_ref,
    mask_ref,
    o_out,
    dq_out,
    dk_out,
    dv_out,
    gain_out,
    q4,
    do4,
    kraw,
    kbuf,
    vbuf,
    qn,
    qnt,
    dot_t,
    don,
    ut,
    rinv,
    wbuf,
    sbuf,
    vslot,
    kslot,
    vsend,
    ksend,
    vland,
    kland,
    obuf,
    dqbuf,
    gkbuf,
    gvbuf,
    early,
    mirror,
    peer_share,
    kother,
    unit_keys,
    inverse_keys,
    oturn,
    overlap,
    gcol,
    member_gain,
    cross_gain,
    total_gain,
    local_sem,
    swap_send,
    swap_recv,
    ag_send,
    ag_recv,
    rs_send,
    rs_recv,
    out_local,
    out_send,
    out_recv,
    share_sems,
    ready_sem,
    member_send,
    member_recv,
    cross_send,
    cross_recv,
    total_send,
    total_recv,
):
    max_tokens = k_ref.shape[0]
    tokens = q_ref.shape[0]
    half = group * HEAD_DIM
    pair_width = 2 * HEAD_DIM
    pairs = group // 2
    tile_total = 2 * tokens // TEXT_TILE
    subs = max_tokens // TILE_TOK
    scale = HEAD_DIM ** (-0.5)

    seq = lax.axis_index("seq")
    core = lax.rem(seq, 2)
    x = lax.rem(lax.div(seq, 2), RING)
    z = lax.div(seq, 2 * RING)
    other = 1 - core

    def image_at(zz, xx, parity):
        return zz * (2 * RING) + lax.rem(xx + RING, RING) * 2 + parity

    peer = image_at(z, x, other)
    dp = lax.axis_index("dp")
    mp = lax.axis_index("mp")
    right = image_at(z, x + 1, core)
    left = image_at(z, x - 1, core)
    across = image_at(1 - z, x, core)
    chip = image_at(z, x, 0)

    def columns(index, width):
        return pl.ds(pl.multiple_of(index * width, width), width)

    own_rows = columns(core, tokens)
    other_rows = columns(other, tokens)

    def remote(src, dst, send_sem, recv_sem, device):
        device = device if isinstance(device, dict) else {"seq": device}
        return pltpu.make_async_remote_copy(
            src_ref=src,
            dst_ref=dst,
            send_sem=send_sem,
            recv_sem=recv_sem,
            device_id=device,
            device_id_type=MESH,
        )

    barrier = pltpu.get_barrier_semaphore()
    leader = seq == 0
    members = 2 * 2 * RING
    group_total = dp_total * mp_total
    group_place = dp * mp_total + mp

    def cross_device(k):
        place = lax.rem(group_place + k, group_total)
        return {"dp": lax.div(place, mp_total), "mp": lax.rem(place, mp_total)}

    neighbours = (peer, right, left, across)
    for device in neighbours:

        @pl.when(device != 0)
        def _():
            pl.semaphore_signal(barrier, inc=1, device_id={"seq": device}, device_id_type=MESH)

    @pl.when(leader)
    def _():
        for k in range(1, group_total):
            pl.semaphore_signal(barrier, inc=1, device_id=cross_device(k), device_id_type=MESH)

    def enter():
        @pl.when(leader)
        def _():
            pl.semaphore_wait(ready_sem, len(neighbours))

        @pl.when(jnp.logical_not(leader))
        def _():
            pl.semaphore_wait(barrier, len(neighbours))

        for device in neighbours:

            @pl.when(device == 0)
            def _():
                pl.semaphore_signal(
                    ready_sem, inc=1, device_id={"seq": device}, device_id_type=MESH
                )

    mine = [
        pltpu.make_async_copy(k_ref.at[:, columns(core, HEAD_DIM)], kraw.at[core], local_sem.at[0]),
        pltpu.make_async_copy(
            v_ref.at[:, columns(core, HEAD_DIM)], vbuf.at[chip + core], local_sem.at[1]
        ),
        pltpu.make_async_copy(q_ref.at[:, columns(core, half)], q4.at[own_rows], local_sem.at[2]),
        pltpu.make_async_copy(do_ref.at[:, columns(core, half)], do4.at[own_rows], local_sem.at[3]),
        pltpu.make_async_copy(k_ref.at[:, columns(other, HEAD_DIM)], kother, local_sem.at[4]),
    ]
    for copy in mine:
        copy.start()

    swaps = [
        (k_ref.at[:, columns(other, HEAD_DIM)], kraw.at[core]),
        (v_ref.at[:, columns(other, HEAD_DIM)], vbuf.at[chip + core]),
        (q_ref.at[:, columns(other, half)], q4.at[own_rows]),
        (do_ref.at[:, columns(other, half)], do4.at[own_rows]),
    ]
    swaps = [
        remote(src, dst, swap_send.at[i], swap_recv.at[i], peer)
        for i, (src, dst) in enumerate(swaps)
    ]

    tile_base = lax.div(seq, 2) * tile_total
    first, count = [], []
    for t in range(tile_total):
        begin = jnp.int32(images)
        total = jnp.int32(0)
        for i in range(images):
            flag = mask_ref[i, tile_base + t]
            total = total + flag
            begin = jnp.where((flag == 1) & (begin == images), i, begin)
        first.append(begin)
        count.append(total)

    def pick(values, t):
        out = values[0]
        for k in range(1, len(values)):
            out = jnp.where(t == k, values[k], out)
        return out

    def reads(t):
        begin = pick(first, t)
        total = pick(count, t)
        found = []
        for r in range(READ_MOST):
            image = jnp.minimum(begin + r, images - 1)
            length = jnp.where(r < total, tiles_ref[image] * TILE_TOK, 0)
            found.append((image, length))
        return found

    def gather_message(buf, which, number, parity, image, device):
        slot = (number - 1) * 2 + parity
        return remote(
            buf.at[image],
            buf.at[image],
            ag_send.at[which, slot],
            ag_recv.at[which, slot],
            device,
        )

    ahead = jnp.where(core == 0, right, left)
    behind = jnp.where(core == 0, left, right)

    def gather_ahead(buf, which, parity):
        return gather_message(buf, which, 6 + core, parity, chip + parity, ahead)

    def gather_behind(buf, which, parity):
        return gather_message(buf, which, 7 - core, parity, chip + parity, behind)

    def gather_across(buf, which, parity):
        return gather_message(buf, which, 4, parity, chip + parity, across)

    def gather_beside(buf, which, parity):
        device = jnp.where(parity == 0, left, right)
        return gather_message(buf, which, 1, parity, image_at(1 - z, x, parity), device)

    def gather_copy(buf, which, number, parity):
        if number == 6:
            image, device = image_at(z, x, parity), right
        elif number == 7:
            image, device = image_at(z, x, parity), left
        elif number == 4:
            image, device = image_at(z, x, parity), across
        elif number == 5:
            image, device = image_at(z, x - 1 + 2 * parity, parity), (right, left)[parity]
        elif number == 3:
            image, device = image_at(z, x - 1 + 2 * parity, parity), across
        elif number == 1:
            image, device = image_at(1 - z, x, parity), (left, right)[parity]
        else:
            image, device = image_at(1 - z, x + 1 - 2 * parity, parity), (left, right)[parity]
        return gather_message(buf, which, number, parity, image, device)

    def gather_own(buf, which):
        gather_ahead(buf, which, core).start()
        gather_across(buf, which, core).start()

    def gather_swapped(buf, which):
        gather_behind(buf, which, other).start()
        gather_across(buf, which, other).start()
        gather_ahead(buf, which, other).start()
        gather_behind(buf, which, core).start()

    def gather_second(buf, which):
        for parity in (core, other):
            gather_across(buf, which, parity).wait_recv()
            gather_beside(buf, which, parity).start()

    def gather_third(buf, which):
        for parity, source in ((0, 6), (1, 7)):
            gather_copy(buf, which, source, parity).wait_recv()
            gather_copy(buf, which, 5, parity).start()
            gather_copy(buf, which, 3, parity).start()

    def gather_fourth(buf, which):
        for parity in (0, 1):
            gather_copy(buf, which, 1, parity).wait_recv()
            gather_copy(buf, which, 2, parity).start()

    def gather_last(buf, which):
        for number, parity in (
            (6, 1), (7, 0), (5, 0), (5, 1), (3, 0), (3, 1), (2, 0), (2, 1),
        ):
            gather_copy(buf, which, number, parity).wait_recv()
        for number in range(1, 8):
            for parity in (0, 1):
                gather_copy(buf, which, number, parity).wait_send()

    key_gain = gains_ref[1:2, :]

    def norm_rows(entries, place, rows):
        inverse = lax.rsqrt(jnp.mean(entries * entries, axis=-1, keepdims=True) + EPSILON)
        unit = entries * inverse
        if place is not None:
            unit_keys[place, rows, :] = unit
            inverse_keys[place, rows, :] = inverse
        return unit

    def norm_keys(parity, place):
        for s in range(subs):
            rows = slice(s * TILE_TOK, (s + 1) * TILE_TOK)
            unit = norm_rows(kraw[parity, rows, :].astype(F32), place, rows)
            kbuf[chip + parity, rows, :] = (unit * key_gain).astype(BF16)

    mine[0].wait()
    norm_keys(core, core)
    enter()
    swaps[0].start()
    gather_own(kbuf, 0)
    for copy in swaps[1:]:
        copy.start()
    swaps[0].wait_recv()
    norm_keys(other, None)
    gather_swapped(kbuf, 0)

    gcol[...] = jnp.transpose(jnp.broadcast_to(gains_ref[0:1, :], (HEAD_DIM, HEAD_DIM)))
    overlap[...] = jnp.zeros_like(overlap)
    for i in (2, 3):
        mine[i].wait()
        swaps[i].wait_recv()

    def prepare(t, carry):
        rows = columns(t, TEXT_TILE)
        gain_column = gcol[...]
        for h in range(group):
            cols = slice(h * HEAD_DIM, (h + 1) * HEAD_DIM)
            turned = jnp.transpose(q4[rows, cols].astype(F32))
            inverse = lax.rsqrt(jnp.mean(turned * turned, axis=0, keepdims=True) + EPSILON)
            unit = turned * inverse
            normed = unit * gain_column
            ut[t, :, cols] = unit
            rinv[t, :, cols] = inverse
            qnt[t, :, cols] = normed.astype(BF16)
            qn[t, cols, :] = jnp.transpose(normed).astype(BF16)
            cotangent = do4[rows, cols]
            don[t, cols, :] = cotangent
            dot_t[t, :, cols] = jnp.transpose(cotangent.astype(F32)).astype(BF16)

        return carry

    lax.fori_loop(0, tile_total, prepare, 0)

    mine[4].wait()
    for s in range(subs):
        rows = slice(s * TILE_TOK, (s + 1) * TILE_TOK)
        norm_rows(kother[rows, :].astype(F32), other, rows)

    gather_second(kbuf, 0)
    gather_third(kbuf, 0)
    mine[1].wait()
    swaps[1].wait_recv()
    gather_across(vbuf, 1, core).start()
    gather_across(vbuf, 1, other).start()
    gather_fourth(kbuf, 0)
    gather_ahead(vbuf, 1, core).start()
    gather_behind(vbuf, 1, other).start()
    gather_ahead(vbuf, 1, other).start()
    gather_behind(vbuf, 1, core).start()
    gather_last(kbuf, 0)

    def forward(t, carry):
        slots = reads(t)
        keys = [kbuf[image] for image, _ in slots]
        for pair in range(pairs):
            cols = slice(pair * pair_width, (pair + 1) * pair_width)
            turned = qnt[t, :, cols]
            scratch = sbuf.at[pair % 2]
            peak = jnp.full((1, pair_width), -1e30, F32)
            for r, (_, length) in enumerate(slots):
                scores = dot(keys[r], turned)
                scratch[r * max_tokens : (r + 1) * max_tokens, :] = scores
                for s in range(subs):
                    top = jnp.max(scores[s * TILE_TOK : (s + 1) * TILE_TOK], axis=0, keepdims=True)
                    peak = jnp.maximum(peak, jnp.where(s * TILE_TOK < length, top, -1e30))
            total = jnp.zeros((1, pair_width), F32)
            for r, (_, length) in enumerate(slots):
                for s in range(subs):
                    begin = r * max_tokens + s * TILE_TOK
                    shift = jnp.where(s * TILE_TOK < length, peak, 1e30)
                    powers = jnp.exp2(
                        (scratch[begin : begin + TILE_TOK, :] - shift) * (scale * LOG2E)
                    )
                    scratch[begin : begin + TILE_TOK, :] = powers
                    total = total + jnp.sum(powers, axis=0, keepdims=True)
            inverse = 1.0 / total
            for r in range(READ_MOST * subs):
                begin = r * TILE_TOK
                wbuf[t, begin : begin + TILE_TOK, cols] = (
                    scratch[begin : begin + TILE_TOK, :] * inverse
                ).astype(BF16)
        cotangents = don[t]
        for r in range(READ_MOST):
            rows = slice(r * max_tokens, (r + 1) * max_tokens)
            vslot[t, r] = dot(wbuf[t, rows, :], cotangents)

        @pl.when(t == 0)
        def _():
            gather_second(vbuf, 1)
            gather_third(vbuf, 1)

        @pl.when(t == 2)
        def _():
            gather_fourth(vbuf, 1)

        return carry

    lax.fori_loop(0, tile_total, forward, 0)

    def sum_route(number, parity):
        if number == 1:
            return image_at(1 - z, x + 1 - 2 * parity, parity), (right, left)[parity]
        if number == 2:
            return image_at(1 - z, x + 2, parity), (right, left)[parity]
        if number == 3:
            return image_at(1 - z, x - 1 + 2 * parity, parity), across
        if number == 4:
            return image_at(1 - z, x, parity), across
        if number == 5:
            return image_at(z, x + 2, parity), (left, right)[parity]
        if number == 6:
            return image_at(z, x - 1, parity), left
        return image_at(z, x + 1, parity), right

    def sum_copy(send, land, which, number, parity):
        image, device = sum_route(number, parity)
        slot = (number - 1) * 2 + parity
        place = slot
        if which == 1 and number in (4, 6, 7):
            place = (number - 1) * 2 + core
            device = device - core + parity
        return remote(
            send.at[image], land.at[place], rs_send.at[which, slot], rs_recv.at[which, place], device
        )

    def root_wait(send, land, which, number, head):
        place = (number - 1) * 2 + head
        remote(
            send.at[0], land.at[place], rs_send.at[which, 0], rs_recv.at[which, place], across
        ).wait_recv()

    def share(slot_ref, image, s):
        rows = slice(s * TILE_TOK, (s + 1) * TILE_TOK)
        value = None
        for t in range(tile_total):
            place = image - first[t]
            weight = jnp.where((place >= 0) & (place < count[t]), 1.0, 0.0).astype(F32)
            part = slot_ref[t, jnp.clip(place, 0, READ_MOST - 1), rows, :] * weight
            value = part if value is None else value + part
        return value

    def summed(slot_ref, land, image, sources, s):
        value = share(slot_ref, image, s)
        for number, parity in sources:
            slot = (number - 1) * 2 + parity
            value = value + land[slot, s * TILE_TOK : (s + 1) * TILE_TOK, :].astype(F32)
        return value

    def send_sum(slot_ref, send, land, which, number, parity, sources):
        for source_number, source_parity in sources:
            sum_copy(send, land, which, source_number, source_parity).wait_recv()
        image, _ = sum_route(number, parity)
        for s in range(subs):
            rows = slice(s * TILE_TOK, (s + 1) * TILE_TOK)
            send[image, rows, :] = summed(slot_ref, land, image, sources, s).astype(BF16)
        sum_copy(send, land, which, number, parity).start()

    def sum_far(*refs):
        send_sum(*refs, 2, 0, ())
        send_sum(*refs, 2, 1, ())

    def sum_level(*refs):
        send_sum(*refs, 3, 0, ())
        send_sum(*refs, 3, 1, ())

    def sum_middle(*refs):
        send_sum(*refs, 5, 0, ())
        send_sum(*refs, 5, 1, ())

    def sum_beside(*refs):
        send_sum(*refs, 1, 0, ((2, 0),))
        send_sum(*refs, 1, 1, ((2, 1),))

    def sum_near(*refs):
        send_sum(*refs, 7, 0, ())
        send_sum(*refs, 6, 1, ())

    def sum_across(*refs):
        send_sum(*refs, 4, 0, ((1, 0),))
        send_sum(*refs, 4, 1, ((1, 1),))

    def sum_end(*refs):
        send_sum(*refs, 6, 0, ((5, 0), (3, 0)))
        send_sum(*refs, 7, 1, ((5, 1), (3, 1)))

    root_sources = (4, 6, 7)

    root_messages = [(number, parity) for number in root_sources for parity in (0, 1)]

    def sum_last(send, land, which, arriving):
        for number, parity in arriving:
            sum_copy(send, land, which, number, parity).wait_recv()
        for number in range(1, 8):
            for parity in (0, 1):
                sum_copy(send, land, which, number, parity).wait_send()

    value_refs = (vslot, vsend, vland, 0)
    key_refs = (kslot, ksend, kland, 1)
    sum_far(*value_refs)
    sum_level(*value_refs)
    sum_middle(*value_refs)
    gather_last(vbuf, 1)

    def backward(t, carry):
        slots = reads(t)
        values = [vbuf[image] for image, _ in slots]
        values_turned = [jnp.transpose(value) for value in values]
        for pair in range(pairs):
            cols = slice(pair * pair_width, (pair + 1) * pair_width)
            cotangent = dot_t[t, :, cols]
            attended = None
            for r in range(READ_MOST):
                part = dot(
                    values_turned[r], wbuf[t, r * max_tokens : (r + 1) * max_tokens, cols]
                )
                attended = part if attended is None else attended + part
            oturn[t, :, cols] = attended.astype(BF16)
            row_dot = jnp.sum(attended * cotangent.astype(F32), axis=0, keepdims=True)
            for r in range(READ_MOST):
                rows = slice(r * max_tokens, (r + 1) * max_tokens)
                value_scores = dot(values[r], cotangent)
                wbuf[t, rows, cols] = (
                    wbuf[t, rows, cols].astype(F32) * (value_scores - row_dot)
                ).astype(BF16)
        normed = qn[t]
        for r, (image, _) in enumerate(slots):
            rows = slice(r * max_tokens, (r + 1) * max_tokens)
            part = dot(wbuf[t, rows, :], normed)
            kslot[t, r] = part
            product = part * kbuf[image].astype(F32)
            overlap[...] += jnp.sum(product.reshape(max_tokens // 8, 8, HEAD_DIM), axis=0)

        @pl.when(t == 0)
        def _():
            sum_beside(*value_refs)
            sum_near(*value_refs)

        return carry

    lax.fori_loop(0, tile_total, backward, 0)

    def member_copy(member):
        return remote(
            overlap, member_gain.at[member], member_send, member_recv.at[member], 0
        )

    def cross_copy(place, k):
        return remote(
            cross_gain.at[place],
            cross_gain.at[place],
            cross_send.at[k],
            cross_recv.at[place],
            cross_device(k),
        )

    def total_copy(member):
        return remote(total_gain, total_gain, total_send.at[member], total_recv, member)

    def in_order(buf, total):
        value = buf[0]
        for k in range(1, total):
            value = value + buf[k]
        return value

    def lead_gather():
        member_gain[0] = overlap[...]
        for member in range(1, members):
            member_copy(member).wait_recv()
        cross_gain[group_place] = in_order(member_gain, members)
        if group_total > 1:
            pl.semaphore_wait(barrier, group_total - 1)
        for k in range(1, group_total):
            cross_copy(group_place, k).start()

    def lead_spread():
        for k in range(1, group_total):
            cross_copy(lax.rem(group_place + k, group_total), k).wait_recv()
        total_gain[...] = in_order(cross_gain, group_total)
        for member in range(1, members):
            total_copy(member).start()

    @pl.when(jnp.logical_not(leader))
    def _():
        member_copy(seq).start()

    sum_far(*key_refs)
    sum_end(*value_refs)

    pl.when(leader)(lead_gather)

    sum_across(*value_refs)
    sum_middle(*key_refs)
    sum_level(*key_refs)

    def queries_backward(t, carry):
        slots = reads(t)
        gain_column = gcol[...]
        gain_pair = jnp.concatenate([gain_column, gain_column], axis=1)
        keys_turned = [jnp.transpose(kbuf[image]) for image, _ in slots]
        rows_out = columns(t, TEXT_TILE)
        for pair in range(pairs):
            cols = slice(pair * pair_width, (pair + 1) * pair_width)
            grads = None
            for r in range(READ_MOST):
                part = dot(keys_turned[r], wbuf[t, r * max_tokens : (r + 1) * max_tokens, cols])
                grads = part if grads is None else grads + part
            grads = grads * scale
            unit = ut[t, :, cols]
            scaled = grads * gain_pair
            mean = jnp.mean(scaled * unit, axis=0, keepdims=True)
            grad_query = rinv[t, :, cols] * (scaled - unit * mean)
            for h in range(2):
                head = slice(h * HEAD_DIM, (h + 1) * HEAD_DIM)
                out_cols = slice((2 * pair + h) * HEAD_DIM, (2 * pair + h + 1) * HEAD_DIM)
                obuf[rows_out, out_cols] = jnp.transpose(oturn[t, :, out_cols])
                dqbuf[rows_out, out_cols] = jnp.transpose(grad_query[:, head]).astype(BF16)

        @pl.when(t == 1)
        def _():
            sum_beside(*key_refs)
            sum_near(*key_refs)

        return carry

    lax.fori_loop(0, tile_total, queries_backward, 0)

    out_cols = columns(core, half)
    head_cols = columns(core, HEAD_DIM)
    results = [
        (obuf.at[own_rows], obuf.at[other_rows], o_out, out_cols),
        (dqbuf.at[own_rows], dqbuf.at[other_rows], dq_out, out_cols),
        (gvbuf.at[core], gvbuf.at[other], dv_out, head_cols),
    ]
    locals_out = [
        pltpu.make_async_copy(own, out.at[:, cols], out_local.at[i])
        for i, (own, _, out, cols) in enumerate(results)
    ]
    remotes_out = [
        remote(theirs, out.at[:, cols], out_send.at[i], out_recv.at[i], peer)
        for i, (_, theirs, out, cols) in enumerate(results)
    ]

    def put_out(i):
        locals_out[i].start()
        remotes_out[i].start()

    put_out(0)
    put_out(1)

    def root_sum(slot_ref, land, parity, s):
        sources = [(number, parity) for number in root_sources]
        return summed(slot_ref, land, chip + parity, sources, s)

    sum_last(vsend, vland, 0, root_messages)
    for parity in (other, core):
        for s in range(subs):
            rows = slice(s * TILE_TOK, (s + 1) * TILE_TOK)
            gvbuf[parity, rows, :] = root_sum(vslot, vland, parity, s).astype(BF16)
    put_out(2)

    pl.when(leader)(lead_spread)

    for s in range(subs):
        rows = slice(s * TILE_TOK, (s + 1) * TILE_TOK)
        mirror[rows, :] = share(kslot, chip + other, s)
        early[core, rows, :] = share(kslot, chip + core, s)
    share_copy = remote(mirror, peer_share, share_sems.at[0], share_sems.at[1], peer)
    share_copy.start()
    sum_across(*key_refs)
    sum_end(*key_refs)
    share_copy.wait()
    near, late = 7 - core, 6 + core
    for head in (0, 1):
        root_wait(ksend, kland, 1, near, head)
    for s in range(subs):
        rows = slice(s * TILE_TOK, (s + 1) * TILE_TOK)
        place = (near - 1) * 2
        early[core, rows, :] += kland[place + core, rows, :].astype(F32)
        early[other, rows, :] = peer_share[rows, :] + kland[place + other, rows, :].astype(F32)
    for number in (4, late):
        for head in (0, 1):
            root_wait(ksend, kland, 1, number, head)
    sum_last(ksend, kland, 1, ())
    last_out = []
    for head in (0, 1):
        for s in range(subs):
            rows = slice(s * TILE_TOK, (s + 1) * TILE_TOK)
            grads = early[head, rows, :]
            for number in (4, late):
                grads = grads + kland[(number - 1) * 2 + head, rows, :].astype(F32)
            grads = grads * scale
            unit = unit_keys[head, rows, :]
            scaled = grads * key_gain
            mean = jnp.mean(scaled * unit, axis=-1, keepdims=True)
            gkbuf[head, rows, :] = (
                inverse_keys[head, rows, :] * (scaled - unit * mean)
            ).astype(BF16)
        last_out.append(
            pltpu.make_async_copy(
                gkbuf.at[head],
                dk_out.at[:, head * HEAD_DIM : (head + 1) * HEAD_DIM],
                out_local.at[3 + head],
            )
        )
        last_out[head].start()
    @pl.when(jnp.logical_not(leader))
    def _():
        total_copy(0).wait_recv()
        member_copy(seq).wait_send()

    @pl.when(leader)
    def _():
        for k in range(1, group_total):
            cross_copy(group_place, k).wait_send()
        for member in range(1, members):
            total_copy(member).wait_send()

    products = jnp.sum(total_gain[...], axis=0, keepdims=True) * scale
    gain_out[...] = products / gains_ref[...]

    for copy in swaps:
        copy.wait_send()
    for copy in last_out:
        copy.wait()
    for i in range(len(results)):
        locals_out[i].wait()
        remotes_out[i].wait_send()
        remotes_out[i].wait_recv()


def mover(count, *refs):
    sources, targets = refs[:count], refs[count : 2 * count]
    stages, load_sem, store_sem = refs[2 * count : 3 * count], refs[-2], refs[-1]
    loads, stores = [], []
    for source, stage, target in zip(sources, stages, targets):
        cuts = MOVE_CUTS if source.shape[0] % (16 * MOVE_CUTS) == 0 else 1
        rows = source.shape[0] // cuts
        for k in range(cuts):
            cut = pl.ds(k * rows, rows)
            place = len(loads)
            loads.append(pltpu.make_async_copy(source.at[cut], stage.at[cut], load_sem.at[place]))
            stores.append(pltpu.make_async_copy(stage.at[cut], target.at[cut], store_sem.at[place]))
    for load in loads:
        load.start()
    for load, store in zip(loads, stores):
        load.wait()
        store.start()
    for store in stores:
        store.wait()


def on_device(
    dp_total,
    mp_total,
    queries,
    image_keys,
    image_values,
    norm_gains,
    image_tiles,
    read_mask,
    grad_attended,
):
    tokens, width = queries.shape[1:]
    max_tokens, kv_width = image_keys.shape[2:]
    group = width // kv_width
    images = read_mask.shape[2]
    half = group * HEAD_DIM
    tile_total = 2 * tokens // TEXT_TILE
    slot_width = READ_MOST * max_tokens
    hbm = pl.BlockSpec(memory_space=pl.ANY)
    vmem = pl.BlockSpec(memory_space=pltpu.VMEM)
    smem = pl.BlockSpec(memory_space=pltpu.SMEM)
    dma = pltpu.SemaphoreType.DMA
    block = (images, max_tokens, HEAD_DIM)
    slots = (tile_total, READ_MOST, max_tokens, HEAD_DIM)
    turned = (tile_total, HEAD_DIM, half)
    plain = (tile_total, half, HEAD_DIM)
    scratch = [
        pltpu.VMEM((2 * tokens, half), BF16),
        pltpu.VMEM((2 * tokens, half), BF16),
        pltpu.VMEM((2, max_tokens, HEAD_DIM), BF16),
        pltpu.VMEM(block, BF16),
        pltpu.VMEM(block, BF16),
        pltpu.VMEM(plain, BF16),
        pltpu.VMEM(turned, BF16),
        pltpu.VMEM(turned, BF16),
        pltpu.VMEM(plain, BF16),
        pltpu.VMEM(turned, F32),
        pltpu.VMEM((tile_total, 1, half), F32),
        pltpu.VMEM((tile_total, slot_width, half), BF16),
        pltpu.VMEM((2, slot_width, 2 * HEAD_DIM), F32),
        pltpu.VMEM(slots, F32),
        pltpu.VMEM(slots, F32),
        pltpu.VMEM(block, BF16),
        pltpu.VMEM(block, BF16),
        pltpu.VMEM((14, max_tokens, HEAD_DIM), BF16),
        pltpu.VMEM((14, max_tokens, HEAD_DIM), BF16),
        pltpu.VMEM((2 * tokens, half), BF16),
        pltpu.VMEM((2 * tokens, half), BF16),
        pltpu.VMEM((2, max_tokens, HEAD_DIM), BF16),
        pltpu.VMEM((2, max_tokens, HEAD_DIM), BF16),
        pltpu.VMEM((2, max_tokens, HEAD_DIM), F32),
        pltpu.VMEM((max_tokens, HEAD_DIM), F32),
        pltpu.VMEM((max_tokens, HEAD_DIM), F32),
        pltpu.VMEM((max_tokens, HEAD_DIM), BF16),
        pltpu.VMEM((2, max_tokens, HEAD_DIM), F32),
        pltpu.VMEM((2, max_tokens, 1), F32),
        pltpu.VMEM(turned, BF16),
        pltpu.VMEM((8, HEAD_DIM), F32),
        pltpu.VMEM((HEAD_DIM, HEAD_DIM), F32),
        pltpu.VMEM((4 * RING, 8, HEAD_DIM), F32),
        pltpu.VMEM((dp_total * mp_total, 8, HEAD_DIM), F32),
        pltpu.VMEM((8, HEAD_DIM), F32),
        dma((5,)),
        dma((5,)),
        dma((5,)),
        dma((2, 14)),
        dma((2, 14)),
        dma((2, 14)),
        dma((2, 14)),
        dma((5,)),
        dma((4,)),
        dma((4,)),
        dma((2,)),
        pltpu.SemaphoreType.REGULAR,
        dma(()),
        dma((4 * RING,)),
        dma((dp_total * mp_total,)),
        dma((dp_total * mp_total,)),
        dma((4 * RING,)),
        dma(()),
    ]
    attended, grad_queries, grad_keys, grad_values, grad_gains = pl.pallas_call(
        functools.partial(kernel, images, group, dp_total, mp_total),
        out_shape=[
            jax.ShapeDtypeStruct((tokens, width), BF16),
            jax.ShapeDtypeStruct((tokens, width), BF16),
            jax.ShapeDtypeStruct((max_tokens, kv_width), BF16),
            jax.ShapeDtypeStruct((max_tokens, kv_width), BF16),
            jax.ShapeDtypeStruct((2, HEAD_DIM), F32),
        ],
        in_specs=[hbm, hbm, hbm, hbm, vmem, smem, smem],
        out_specs=[hbm, hbm, hbm, hbm, vmem],
        scratch_shapes=scratch,
        compiler_params=pltpu.CompilerParams(
            collective_id=0, has_side_effects=True, vmem_limit_bytes=60 * 1024 * 1024
        ),
    )(
        queries[0],
        grad_attended[0],
        image_keys[0, 0],
        image_values[0, 0],
        norm_gains,
        image_tiles[0],
        jnp.transpose(read_mask[0]),
    )
    results = (attended, grad_queries, grad_keys, grad_values, grad_gains)
    attended, grad_queries, grad_keys, grad_values, grad_gains = pl.pallas_call(
        functools.partial(mover, len(results)),
        out_shape=[jax.ShapeDtypeStruct(part.shape, part.dtype) for part in results],
        in_specs=[hbm] * len(results),
        out_specs=[hbm] * len(results),
        scratch_shapes=[pltpu.VMEM(part.shape, part.dtype) for part in results]
        + [dma((MOVE_CUTS * len(results),))] * 2,
        compiler_params=pltpu.CompilerParams(vmem_limit_bytes=60 * 1024 * 1024),
    )(*results)
    return (
        attended[None],
        grad_queries[None],
        grad_keys[None, None],
        grad_values[None, None],
        grad_gains,
    )


def solution(mesh):
    in_specs = (
        P("dp", "seq", "mp"),
        P("dp", "seq", None, "mp"),
        P("dp", "seq", None, "mp"),
        P(),
        P("dp", None),
        P("dp", None, None),
        P("dp", "seq", "mp"),
    )
    out_specs = (
        P("dp", "seq", "mp"),
        P("dp", "seq", "mp"),
        P("dp", "seq", None, "mp"),
        P("dp", "seq", None, "mp"),
        P(),
    )
    per_device = functools.partial(on_device, mesh.shape["dp"], mesh.shape["mp"])
    return jax.shard_map(
        per_device, mesh=mesh, in_specs=in_specs, out_specs=out_specs, check_vma=False
    )
```
